512 devices in a mesh: ctx: 64 (over x, z), dp: 8 (over y, core).
Axes of the slice: x: 4, y: 4, z: 16, core: 2. Of those that a mesh axis runs over, the one named last changes fastest.
Arguments:
- queries: bfloat16 [32768, 4096], P('ctx', 'dp'), may hold values from -6 to 6
- keys: bfloat16 [32768, 4096], P('ctx', 'dp'), may hold values from -0.5 to 0.5
- values: bfloat16 [32768, 4096], P('ctx', 'dp'), may hold values from -6 to 6
- cotangent: bfloat16 [32768, 4096], P('ctx', 'dp'), may hold values from -6 to 6
- log_decay: float32 [32], P('dp'), may hold values from 6.1035156e-06 to 0.04
- gain: float32 [4096], P(('dp', 'ctx')), may hold values from 0.1 to 1.9
Outputs:
- normed: bfloat16 [32768, 4096], P('ctx', 'dp')
- grad_queries: bfloat16 [32768, 4096], P('ctx', 'dp')
- grad_keys: bfloat16 [32768, 4096], P('ctx', 'dp')
- grad_values: bfloat16 [32768, 4096], P('ctx', 'dp')
- grad_gain: float32 [4096], P(('dp', 'ctx'))
The draws below stay inside these ranges and needn't reach their ends.
All inputs are finite; a program needn't handle non-finite values.
Results may differ from the reference program's by a relative error of at most 0.0065.
Values may be sent and summed in bfloat16 or wider, within the bound.
A program may use at most 128 MiB of HBM per device.

```python
import math
import jax
import jax.numpy as jnp
from jax import lax

HEAD = 128
HEADS = 32
TOK_DEV = 512
TOKENS = 32768


def draw_log_decay(key, part):
    key = jax.random.fold_in(key, 7)
    first_key, second_key, third_key = jax.random.split(key, 3)
    slow_share = 0.5
    picker = jax.random.uniform(first_key, (HEADS,), jnp.float32)
    slow_rates = jnp.exp(jax.random.uniform(second_key, (HEADS,), jnp.float32, math.log(0.2 / TOKENS), math.log(2.0 / TOKENS)))
    fast_rates = jnp.exp(jax.random.uniform(third_key, (HEADS,), jnp.float32, math.log(1.0 / 60.0), math.log(0.04)))
    return jnp.where(picker < slow_share, slow_rates, fast_rates).astype(jnp.float32)


def block_scale(rng, extent, cuts, smallest, top_value):
    def one(position, shards_of):
        draws = jax.random.uniform(jax.random.fold_in(jax.random.fold_in(rng, 6), position), (shards_of,), jnp.float32, smallest / len(cuts), top_value / len(cuts))
        return jnp.repeat(jnp.exp(draws), extent[position] // shards_of).reshape((-1,) + (1,) * (len(extent) - position - 1))

    factor_of = one(*cuts[0])
    for cut in cuts[1:]:
        factor_of = factor_of * one(*cut)
    return factor_of


def gaussian(own_key, dims, scale, reach, shards=(), held_as=jnp.bfloat16):
    level = block_scale(own_key, dims, shards, -0.22, 0.18) if shards else 1.0
    values = jax.random.normal(own_key, dims, jnp.float32) * scale * level
    return jnp.minimum(jnp.maximum(values, -reach), reach).astype(held_as)


def setup_inputs(seed: int = 0) -> dict:
    streams_of = jax.random.split(jax.random.key(seed), 7)
    queries = gaussian(streams_of[0], (TOKENS, HEADS * HEAD), 1.0, 6.0, ((0, 64), (1, 8)))
    keys = gaussian(streams_of[1], (TOKENS, HEADS * HEAD), HEAD ** -0.5, 0.5, ((0, 64), (1, 8)))
    values = gaussian(streams_of[2], (TOKENS, HEADS * HEAD), 1.0, 6.0, ((0, 64), (1, 8)))
    cotangent = gaussian(streams_of[3], (TOKENS, HEADS * HEAD), 1.0, 6.0, ((0, 64), (1, 8)))
    log_decay = draw_log_decay(jax.random.fold_in(streams_of[6], 71), 0)
    gain = jnp.clip(1.0 + 0.18 * jax.random.normal(streams_of[5], (HEADS * HEAD,), jnp.float32), 0.1, 1.9)
    return dict(queries=queries, keys=keys, values=values, cotangent=cotangent, log_decay=log_decay, gain=gain)


eps_norm = 1e-06

def to_bfloat(values_in):
    return lax.optimization_barrier(values_in.astype(jnp.bfloat16)).astype(jnp.float32)

def decay_tables(log_decay, length):
    places = jnp.arange(length, dtype=jnp.float32)
    offsets = places[:, None] - places[None, :]
    rates = log_decay[:, None, None]
    decay_mask = jnp.where(offsets[None] >= 0.0, jnp.exp(-rates * jnp.maximum(offsets, 0.0)[None]), 0.0)
    from_start = jnp.exp(-log_decay[None, :] * (places[:, None] + 1.0))
    into_block = jnp.exp(-log_decay[None, :] * (length - 1.0 - places[:, None]))
    back_weight = jnp.exp(-log_decay[None, :] * places[:, None])
    back_rest = jnp.exp(-log_decay[None, :] * (length - places[:, None]))
    return (decay_mask, from_start[:, :, None], into_block[:, :, None], back_weight[:, :, None], back_rest[:, :, None])

def reference(queries, keys, values, cotangent, log_decay, gain):
    length = TOK_DEV
    heads = HEADS
    width = HEAD
    channels = heads * width
    blocks = TOKENS // length
    shape = (blocks, length, heads, width)
    query_all = queries.reshape(shape)
    key_all = keys.reshape(shape)
    value_all = values.reshape(shape)
    cot_all = cotangent.reshape(shape)
    decay_mask, from_start, into_block, back_weight, back_rest = decay_tables(log_decay, length)
    total = jnp.exp(-log_decay * length)[:, None, None]
    gains = gain.reshape(heads, width)

    def forward(carry, block):
        state, gain_sum = carry
        query_blk, key_blk, value_blk, cot_blk = block
        query_f = query_blk.astype(jnp.float32)
        key_f = key_blk.astype(jnp.float32)
        value_f = value_blk.astype(jnp.float32)
        probs = to_bfloat(jnp.einsum('thd,ihd->hti', query_f, key_f) * decay_mask)
        local_out = jnp.einsum('hti,ihe->the', probs, value_f)
        state_b = state.astype(jnp.bfloat16)
        attn = local_out + from_start * jnp.einsum('thd,hde->the', query_f, state_b.astype(jnp.float32))
        inverse = lax.rsqrt(lax.optimization_barrier(jnp.sum(attn * attn, axis=(1, 2))) / channels + eps_norm)[:, None, None]
        cot = cot_blk.astype(jnp.float32)
        cross = lax.optimization_barrier(jnp.sum(cot * gains * attn, axis=(1, 2)))[:, None, None]
        normed = (attn * inverse * gains).astype(jnp.bfloat16)
        grad_attn = (cot * gains * inverse - attn * inverse ** 3 * cross / channels).astype(jnp.bfloat16)
        gain_sum = gain_sum + lax.optimization_barrier(jnp.sum(cot * attn * inverse, axis=0))
        key_weighted = to_bfloat(key_f * into_block)
        block_state = jnp.einsum('thd,the->hde', key_weighted, value_f)
        return ((total * state + block_state, gain_sum), (normed, grad_attn, state_b))
    start = (jnp.zeros((heads, width, width), jnp.float32), jnp.zeros((heads, width), jnp.float32))
    (last_state, gain_sum), (normed, grad_attn, state_bs) = lax.scan(forward, start, (query_all, key_all, value_all, cot_all))

    def backward(state, block):
        query_blk, key_blk, value_blk, grad_blk, state_b = block
        query_f = query_blk.astype(jnp.float32)
        key_f = key_blk.astype(jnp.float32)
        value_f = value_blk.astype(jnp.float32)
        grad_f = grad_blk.astype(jnp.float32)
        probs = to_bfloat(jnp.einsum('thd,ihd->hti', query_f, key_f) * decay_mask)
        dscore = to_bfloat(jnp.einsum('the,ihe->hti', grad_f, value_f) * decay_mask)
        later_b = to_bfloat(state)
        incoming_b = state_b.astype(jnp.float32)
        grad_q = jnp.einsum('hti,ihd->thd', dscore, key_f) + from_start * jnp.einsum('the,hde->thd', grad_f, incoming_b)
        grad_k = jnp.einsum('hti,thd->ihd', dscore, query_f) + back_rest * jnp.einsum('ihe,hde->ihd', value_f, later_b)
        grad_v = jnp.einsum('hti,the->ihe', probs, grad_f) + back_rest * jnp.einsum('ihd,hde->ihe', key_f, later_b)
        query_weighted = to_bfloat(query_f * back_weight)
        back_state = jnp.einsum('thd,the->hde', query_weighted, grad_f)
        outs = (grad_q.astype(jnp.bfloat16), grad_k.astype(jnp.bfloat16), grad_v.astype(jnp.bfloat16))
        return (total * state + back_state, outs)
    zero_state = jnp.zeros((heads, width, width), jnp.float32)
    final_back, (grad_q, grad_k, grad_v) = lax.scan(backward, zero_state, (query_all, key_all, value_all, grad_attn, state_bs), reverse=True)
    flat = (TOKENS, channels)
    return (normed.reshape(flat), grad_q.reshape(flat), grad_k.reshape(flat), grad_v.reshape(flat), gain_sum.reshape(-1))
```

```python
import functools

import jax
import jax.numpy as jnp
from jax import lax
from jax.experimental import pallas as pl
from jax.experimental.pallas import tpu as pltpu
from jax.sharding import PartitionSpec as P

HEAD = 128
LOCAL = 4
TOK = 512
WIDE = LOCAL * HEAD
SUB = 128
BLOCKS = TOK // SUB
HALF = 256
X = 4
PAIR = 2 * HEAD

eps_norm = 1e-06
F32, BF16 = jnp.float32, jnp.bfloat16
MESH = pl.DeviceIdType.MESH
HIGH = lax.Precision.HIGHEST


def dot(a, b, over_a, over_b, precision=None):
    return lax.dot_general(
        a, b, (((over_a,), (over_b,)), ((), ())), precision=precision, preferred_element_type=F32
    )


def each_peer(count, me, body):
    def step(i, carry):
        offset = count // 2 + ((i + 1) // 2) * (1 - 2 * lax.rem(i, 2))
        body(lax.rem(me + offset, count))
        return carry

    lax.fori_loop(0, count - 1, step, 0)


def wait_for(ref, sem):
    pltpu.make_async_copy(ref, ref, sem).wait()


class Scan:
    def __init__(self, place, rate_ref, backward, refs):
        self.x, self.z, self.Z = place
        self.rate_ref = rate_ref
        self.backward = backward
        self.send, self.gather, self.pre, self.totals, self.back, self.result, self.sems = refs
        self.rows = PAIR // self.Z

    def sem(self, kind, j):
        return self.sems.at[kind, j]

    def rate(self, j):
        return self.rate_ref[2 * j + self.z // (self.Z // 2)]

    def exchange(self, j):
        rows, z = self.rows, self.z

        def one(peer):
            pltpu.make_async_remote_copy(
                src_ref=self.send.at[pl.ds(pl.multiple_of(j * PAIR + peer * rows, rows), rows)],
                dst_ref=self.gather.at[j, z],
                send_sem=self.sem(0, j),
                recv_sem=self.sem(1, j),
                device_id={"ctx": self.x * self.Z + peer},
                device_id_type=MESH,
            ).start()

        each_peer(self.Z, z, one)
        own = self.send[pl.ds(pl.multiple_of(j * PAIR + z * rows, rows), rows)]
        self.gather[j, z] = own

    def total(self, j):
        rows, x = self.rows, self.x
        wait_for(self.gather.at[j, pl.ds(0, self.Z - 1)], self.sem(1, j))
        decay = jnp.exp(jnp.full((rows, HEAD), -float(TOK) * self.rate(j), F32))
        state = jnp.zeros((rows, HEAD), F32)
        order = range(self.Z - 1, -1, -1) if self.backward else range(self.Z)
        for place in order:
            self.pre[j, place] = state
            state = decay * state + self.gather[j, place].astype(F32)
        self.totals[j, x] = state

        def one(peer):
            pltpu.make_async_remote_copy(
                src_ref=self.totals.at[j, x],
                dst_ref=self.totals.at[j, x],
                send_sem=self.sem(2, j),
                recv_sem=self.sem(3, j),
                device_id={"ctx": peer * self.Z + self.z},
                device_id_type=MESH,
            ).start()

        each_peer(X, x, one)

    def finish(self, j):
        rows, x, z = self.rows, self.x, self.z
        wait_for(self.totals.at[j, pl.ds(0, X - 1)], self.sem(3, j))
        rate = self.rate(j)
        far = jnp.zeros((rows, HEAD), F32)
        for other in range(X):
            steps = (other - x - 1) if self.backward else (x - other - 1)
            reach = jnp.maximum(steps, 0).astype(F32) * (float(TOK) * self.Z)
            weight = jnp.exp(jnp.full((rows, HEAD), -reach * rate, F32))
            far = far + jnp.where(steps >= 0, weight * self.totals[j, other], 0.0)
        decay = jnp.exp(jnp.full((rows, HEAD), -float(TOK) * rate, F32))
        order = range(self.Z - 1, -1, -1) if self.backward else range(self.Z)
        for place in order:
            self.back[j, place] = (self.pre[j, place] + far).astype(BF16)
            far = far * decay

        def one(peer):
            pltpu.make_async_remote_copy(
                src_ref=self.back.at[j, peer],
                dst_ref=self.result.at[pl.ds(pl.multiple_of(j * PAIR + z * rows, rows), rows)],
                send_sem=self.sem(4, j),
                recv_sem=self.sem(5, j),
                device_id={"ctx": x * self.Z + peer},
                device_id_type=MESH,
            ).start()

        each_peer(self.Z, z, one)
        self.result[pl.ds(pl.multiple_of(j * PAIR + z * rows, rows), rows)] = self.back[j, z]

    def arrived(self, j):
        wait_for(self.back.at[j, pl.ds(0, self.Z - 1)], self.sem(5, j))

    def close(self):
        for j in range(2):
            wait_for(self.gather.at[j, pl.ds(0, self.Z - 1)], self.sem(0, j))
            wait_for(self.totals.at[j, pl.ds(0, X - 1)], self.sem(2, j))
            wait_for(self.back.at[j, pl.ds(0, self.Z - 1)], self.sem(4, j))


def kernel(
    Z,
    DP,
    rate_ref,
    gain_ref,
    q_hbm,
    k_hbm,
    v_hbm,
    cot_hbm,
    normed,
    gq,
    gk,
    gv,
    gg_ref,
    q,
    k,
    v,
    cot,
    grad,
    weighted,
    probs,
    dscore,
    mask,
    down_base,
    up_base,
    attn,
    gk_part,
    gv_part,
    norm_parts,
    gain_z,
    gain_x,
    term,
    term_x,
    term_z,
    *rest,
):
    forward_refs, backward_refs = rest[0:7], rest[7:14]
    load_sems, small_sems = rest[14:]
    ctx, d = lax.axis_index("ctx"), lax.axis_index("dp")
    x, z = ctx // Z, lax.rem(ctx, Z)
    channels = DP * WIDE
    share = WIDE // (X * Z)

    loads = [
        pltpu.make_async_copy(source, target, load_sems.at[i])
        for i, (source, target) in enumerate(
            ((k_hbm, k), (v_hbm, v), (q_hbm, q), (cot_hbm, cot))
        )
    ]
    for load in loads:
        load.start()

    barrier = pltpu.get_barrier_semaphore()

    def greet_row(peer):
        pl.semaphore_signal(
            barrier, inc=1, device_id={"ctx": x * Z + peer}, device_id_type=MESH
        )

    def greet_rows(peer):
        pl.semaphore_signal(
            barrier, inc=1, device_id={"ctx": peer * Z + z}, device_id_type=MESH
        )

    def greet_dp(peer):
        pl.semaphore_signal(barrier, inc=1, device_id={"dp": peer}, device_id_type=MESH)

    each_peer(Z, z, greet_row)
    each_peer(X, x, greet_rows)
    each_peer(DP, d, greet_dp)

    place = (x, z, Z)
    ahead = Scan(place, rate_ref, False, forward_refs)
    behind = Scan(place, rate_ref, True, backward_refs)
    incoming, later = ahead.result, behind.result

    def lanes(h):
        return slice(h * HEAD, (h + 1) * HEAD)

    def rows_of(b):
        return slice(b * SUB, (b + 1) * SUB)

    def scaled(h, count):
        return jnp.exp(jnp.full((1, HEAD), -float(count) * rate_ref[h], F32))

    row_index = lax.broadcasted_iota(jnp.int32, (SUB, HEAD), 0).astype(F32)

    def make_up(h):
        up_base[h] = jnp.exp(-rate_ref[h] * (SUB - 1.0 - row_index))

    def make_down(h):
        down_base[h] = jnp.exp(-rate_ref[h] * row_index)

    def up(h, b, extra=0):
        return up_base[h] * scaled(h, SUB * (BLOCKS - 1 - b) + extra)

    def down(h, b, extra=0):
        return down_base[h] * scaled(h, SUB * b + extra)

    def make_mask(h):
        t = lax.broadcasted_iota(jnp.int32, (HALF, HALF), 0)
        i = lax.broadcasted_iota(jnp.int32, (HALF, HALF), 1)
        offset = (t - i).astype(F32)
        near = jnp.exp(-rate_ref[h] * jnp.maximum(offset, 0.0))
        mask[h, 0] = jnp.where(t >= i, near, 0.0)
        mask[h, 1] = jnp.exp(-rate_ref[h] * (offset + float(HALF)))

    def block_state(h):
        make_up(h)
        weighted_k = jnp.concatenate(
            [
                (k[rows_of(b), lanes(h)].astype(F32) * up(h, b)).astype(BF16)
                for b in range(BLOCKS)
            ],
            axis=0,
        )
        state = dot(weighted_k, v[:, lanes(h)], 0, 0)
        ahead.send[pl.ds(h * HEAD, HEAD)] = state.astype(BF16)

    def masked(h, left, right, out):
        for tb in range(2):
            rows = slice(tb * HALF, (tb + 1) * HALF)
            for ib in range(tb + 1):
                cols = slice(ib * HALF, (ib + 1) * HALF)
                score = dot(left[rows, lanes(h)], right[cols, lanes(h)], 1, 1)
                out[h, rows, cols] = (score * mask[h, tb - ib]).astype(BF16)

    def below(table, h, right):
        return (
            dot(table[h, 0:HALF, 0:HALF], right[0:HALF, lanes(h)], 1, 0),
            dot(table[h, HALF:TOK, :], right[:, lanes(h)], 1, 0),
        )

    def above(table, h, right):
        return (
            dot(table[h, :, 0:HALF], right[:, lanes(h)], 0, 0),
            dot(table[h, HALF:TOK, HALF:TOK], right[HALF:TOK, lanes(h)], 0, 0),
        )

    def local_part(h):
        make_mask(h)
        masked(h, q, k, probs)
        first, second = below(probs, h, v)
        attn[0:HALF, lanes(h)] = first
        attn[HALF:TOK, lanes(h)] = second

    def weigh_queries(h):
        make_down(h)
        for b in range(BLOCKS):
            weighted[rows_of(b), lanes(h)] = (
                q[rows_of(b), lanes(h)].astype(F32) * down(h, b)
            ).astype(BF16)

    def add_remote(h):
        remote = dot(q[:, lanes(h)], incoming[pl.ds(h * HEAD, HEAD)], 1, 0)
        for b in range(BLOCKS):
            attn[rows_of(b), lanes(h)] += down(h, b, 1) * remote[rows_of(b)]

    def send_row(source, target, kind, peer_ctx):
        pltpu.make_async_remote_copy(
            src_ref=source,
            dst_ref=target,
            send_sem=small_sems.at[kind],
            recv_sem=small_sems.at[kind + 1],
            device_id={"ctx": peer_ctx},
            device_id_type=MESH,
        ).start()

    lane = lax.broadcasted_iota(jnp.int32, (1, HEAD), 1)

    def gather_gain():
        own = jnp.zeros((1, HEAD), F32)
        for n in range(share):
            own = jnp.where(lane == z * share + n, gain_ref[n], own)
        gain_z[z] = own
        each_peer(Z, z, lambda peer: send_row(gain_z.at[z], gain_z.at[z], 0, x * Z + peer))

    def spread_gain():
        wait_for(gain_z.at[pl.ds(0, Z - 1)], small_sems.at[1])
        whole = gain_z[0]
        for n in range(1, Z):
            whole = whole + gain_z[n]
        gain_x[x] = whole
        each_peer(X, x, lambda peer: send_row(gain_x.at[x], gain_x.at[x], 2, peer * Z + z))

    def gain_arrived():
        wait_for(gain_x.at[pl.ds(0, X - 1)], small_sems.at[3])

    loads[0].wait()
    loads[1].wait()
    block_state(0)
    block_state(1)
    pl.semaphore_wait(barrier, (Z - 1) + (X - 1) + (DP - 1))
    ahead.exchange(0)
    block_state(2)
    block_state(3)
    ahead.exchange(1)
    gather_gain()
    loads[2].wait()
    local_part(0)
    local_part(1)
    ahead.total(0)
    weigh_queries(0)
    weigh_queries(1)
    ahead.finish(0)
    ahead.total(1)
    spread_gain()
    local_part(2)
    ahead.finish(1)
    local_part(3)
    weigh_queries(2)
    weigh_queries(3)
    loads[3].wait()
    gain_arrived()
    ahead.arrived(0)
    add_remote(0)
    add_remote(1)
    ahead.arrived(1)
    add_remote(2)
    add_remote(3)

    ones = jnp.ones((8, HEAD), F32)
    row8 = lax.broadcasted_iota(jnp.int32, (8, HEAD), 0)
    sums = jnp.zeros((8, HEAD), F32)
    for b in range(BLOCKS):
        square = jnp.zeros((SUB, HEAD), F32)
        cross = jnp.zeros((SUB, HEAD), F32)
        for h in range(LOCAL):
            a = attn[rows_of(b), lanes(h)]
            square = square + a * a
            cross = cross + cot[rows_of(b), lanes(h)].astype(F32) * gain_x[h] * a
        sums = jnp.where(row8 == b, dot(ones, square, 1, 1, HIGH), sums)
        sums = jnp.where(row8 == b + BLOCKS, dot(ones, cross, 1, 1, HIGH), sums)
    norm_parts[d] = sums

    def send_norm(peer):
        pltpu.make_async_remote_copy(
            src_ref=norm_parts.at[d],
            dst_ref=norm_parts.at[d],
            send_sem=small_sems.at[4],
            recv_sem=small_sems.at[5],
            device_id={"dp": peer},
            device_id_type=MESH,
        ).start()

    each_peer(DP, d, send_norm)
    wait_for(norm_parts.at[pl.ds(0, DP - 1)], small_sems.at[5])
    whole = norm_parts[0]
    for n in range(1, DP):
        whole = whole + norm_parts[n]
    inverse_rows = lax.rsqrt(whole[0:BLOCKS] / channels + eps_norm)
    cross_rows = inverse_rows * inverse_rows * inverse_rows * whole[BLOCKS : 2 * BLOCKS] / channels

    def column(rows, b):
        return jnp.broadcast_to(rows[b : b + 1], (SUB, HEAD)).T

    inverse = [column(inverse_rows, b) for b in range(BLOCKS)]
    cross_part = [column(cross_rows, b) for b in range(BLOCKS)]

    def back_state(h):
        for b in range(BLOCKS):
            at = (rows_of(b), lanes(h))
            grad[at] = (
                cot[at].astype(F32) * gain_x[h] * inverse[b] - attn[at] * cross_part[b]
            ).astype(BF16)
        state = dot(weighted[:, lanes(h)], grad[:, lanes(h)], 0, 0)
        behind.send[pl.ds(h * HEAD, HEAD)] = state.astype(BF16)

    def norm_out(h):
        total = jnp.zeros((1, HEAD), F32)
        for b in range(BLOCKS):
            at = (rows_of(b), lanes(h))
            scaled_attn = attn[at] * inverse[b]
            normed[at] = (scaled_attn * gain_x[h]).astype(BF16)
            total = total + jnp.sum(cot[at].astype(F32) * scaled_attn, axis=0, keepdims=True)
        term[h] = total

    def spread_term():
        each_peer(X, x, lambda peer: send_row(term.at[peer], term_x.at[x], 6, peer * Z + z))
        term_x[x] = term[x]

    def gather_term():
        wait_for(term_x.at[pl.ds(0, X - 1)], small_sems.at[7])
        whole = term_x[0]
        for n in range(1, X):
            whole = whole + term_x[n]
        term_z[z] = whole
        each_peer(Z, z, lambda peer: send_row(term_z.at[z], term_z.at[z], 8, x * Z + peer))

    def finish_term():
        wait_for(term_z.at[pl.ds(0, Z - 1)], small_sems.at[9])
        whole = term_z[0]
        for n in range(1, Z):
            whole = whole + term_z[n]
        source = lax.broadcasted_iota(jnp.int32, (HEAD, HEAD), 0)
        target = lax.broadcasted_iota(jnp.int32, (HEAD, HEAD), 1)
        pick = (source == target + z * share).astype(F32)
        mine = dot(jnp.broadcast_to(whole, (8, HEAD)), pick, 1, 0, HIGH)
        gg_ref[...] = mine[0:1, 0:share]

    def gradient_part(h):
        masked(h, grad, v, dscore)
        near = below(dscore, h, k)
        far = dot(grad[:, lanes(h)], incoming[pl.ds(h * HEAD, HEAD)], 1, 1)
        for b in range(BLOCKS):
            half, inner = divmod(b * SUB, HALF)
            gq[rows_of(b), lanes(h)] = (
                near[half][inner : inner + SUB] + down(h, b, 1) * far[rows_of(b)]
            ).astype(BF16)
        first, second = above(dscore, h, q)
        gk_part[0:HALF, lanes(h)] = first
        gk_part[HALF:TOK, lanes(h)] = second
        first, second = above(probs, h, grad)
        gv_part[0:HALF, lanes(h)] = first
        gv_part[HALF:TOK, lanes(h)] = second

    def add_later(h):
        state = later[pl.ds(h * HEAD, HEAD)]
        for_k = dot(v[:, lanes(h)], state, 1, 1)
        for_v = dot(k[:, lanes(h)], state, 1, 0)
        for b in range(BLOCKS):
            at = (rows_of(b), lanes(h))
            weight = up(h, b, 1)
            gk[at] = (gk_part[at] + weight * for_k[rows_of(b)]).astype(BF16)
            gv[at] = (gv_part[at] + weight * for_v[rows_of(b)]).astype(BF16)

    back_state(0)
    back_state(1)
    behind.exchange(0)
    back_state(2)
    back_state(3)
    behind.exchange(1)
    for h in range(LOCAL):
        norm_out(h)
    spread_term()
    gradient_part(0)
    behind.total(0)
    gather_term()
    gradient_part(1)
    behind.finish(0)
    behind.total(1)
    gradient_part(2)
    behind.finish(1)
    gradient_part(3)
    finish_term()
    behind.arrived(0)
    add_later(0)
    add_later(1)
    behind.arrived(1)
    add_later(2)
    add_later(3)

    ahead.close()
    behind.close()
    wait_for(gain_z.at[pl.ds(0, Z - 1)], small_sems.at[0])
    wait_for(gain_x.at[pl.ds(0, X - 1)], small_sems.at[2])
    wait_for(norm_parts.at[pl.ds(0, DP - 1)], small_sems.at[4])
    wait_for(term_x.at[pl.ds(0, X - 1)], small_sems.at[6])
    wait_for(term_z.at[pl.ds(0, Z - 1)], small_sems.at[8])


def per_device(Z, DP, queries, keys, values, cotangent, log_decay, gain):
    rows = PAIR // Z
    share = gain.shape[0]
    tokens = pltpu.VMEM((TOK, WIDE), BF16)
    wide = pltpu.VMEM((TOK, WIDE), F32)
    square = pltpu.VMEM((LOCAL, TOK, TOK), BF16)
    scan = [
        pltpu.VMEM((WIDE, HEAD), BF16),
        pltpu.VMEM((2, Z, rows, HEAD), BF16),
        pltpu.VMEM((2, Z, rows, HEAD), F32),
        pltpu.VMEM((2, X, rows, HEAD), F32),
        pltpu.VMEM((2, Z, rows, HEAD), BF16),
        pltpu.VMEM((WIDE, HEAD), BF16),
        pltpu.SemaphoreType.DMA((6, 2)),
    ]
    out = jax.ShapeDtypeStruct((TOK, WIDE), BF16)
    smem, hbm = pl.BlockSpec(memory_space=pltpu.SMEM), pl.BlockSpec(memory_space=pltpu.HBM)
    vmem = pl.BlockSpec(memory_space=pltpu.VMEM)
    normed, gq, gk, gv, gg = pl.pallas_call(
        functools.partial(kernel, Z, DP),
        out_shape=[out, out, out, out, jax.ShapeDtypeStruct((1, share), F32)],
        in_specs=[smem, smem, hbm, hbm, hbm, hbm],
        out_specs=[vmem] * 5,
        scratch_shapes=[tokens] * 6
        + [square, square]
        + [
            pltpu.VMEM((LOCAL, 2, HALF, HALF), F32),
            pltpu.VMEM((LOCAL, SUB, HEAD), F32),
            pltpu.VMEM((LOCAL, SUB, HEAD), F32),
        ]
        + [wide] * 3
        + [
            pltpu.VMEM((DP, 8, HEAD), F32),
            pltpu.VMEM((Z, 1, HEAD), F32),
            pltpu.VMEM((X, 1, HEAD), F32),
            pltpu.VMEM((LOCAL, 1, HEAD), F32),
            pltpu.VMEM((X, 1, HEAD), F32),
            pltpu.VMEM((Z, 1, HEAD), F32),
        ]
        + scan
        + scan
        + [
            pltpu.SemaphoreType.DMA((4,)),
            pltpu.SemaphoreType.DMA((10,)),
        ],
        compiler_params=pltpu.CompilerParams(
            collective_id=0, has_side_effects=True, vmem_limit_bytes=40 * 1024 * 1024
        ),
        cost_estimate=pl.CostEstimate(
            flops=2_000_000_000, bytes_accessed=4_200_000, transcendentals=700_000
        ),
    )(log_decay, gain, queries, keys, values, cotangent)
    return normed, gq, gk, gv, gg.reshape(share)


def solution(mesh):
    both = P("ctx", "dp")
    return jax.shard_map(
        functools.partial(per_device, mesh.shape["ctx"] // X, mesh.shape["dp"]),
        mesh=mesh,
        in_specs=(both, both, both, both, P("dp"), P(("dp", "ctx"))),
        out_specs=(both, both, both, both, P(("dp", "ctx"))),
        check_vma=False,
    )
```

```python
import functools

import jax
import jax.numpy as jnp
from jax import lax
from jax.experimental import pallas as pl
from jax.experimental.pallas import tpu as pltpu
from jax.sharding import PartitionSpec as P

HEAD = 128
LOCAL = 4
TOK = 512
WIDE = LOCAL * HEAD
SUB = 128
BLOCKS = TOK // SUB
HALF = 256
X = 4
PAIR = 2 * HEAD

eps_norm = 1e-06
F32, BF16 = jnp.float32, jnp.bfloat16
MESH = pl.DeviceIdType.MESH
HIGH = lax.Precision.HIGHEST


def dot(a, b, over_a, over_b, precision=None):
    return lax.dot_general(
        a, b, (((over_a,), (over_b,)), ((), ())), precision=precision, preferred_element_type=F32
    )


def each_peer(count, me, body):
    for i in range(count - 1):
        offset = count // 2 + ((i + 1) // 2) * (1 - 2 * (i % 2))
        body(lax.rem(me + offset, count))


def wait_for(ref, sem):
    pltpu.make_async_copy(ref, ref, sem).wait()


class Scan:
    def __init__(self, place, rate_ref, backward, refs):
        self.x, self.z, self.Z = place
        self.rate_ref = rate_ref
        self.backward = backward
        self.send, self.gather, self.pre, self.totals, self.back, self.result, self.sems = refs
        self.rows = WIDE // self.Z

    def piece(self, ref, place):
        return ref.at[pl.ds(pl.multiple_of(place * self.rows, self.rows), self.rows)]

    def rate(self):
        return self.rate_ref[self.z // (self.Z // LOCAL)]

    def order(self):
        return range(self.Z - 1, -1, -1) if self.backward else range(self.Z)

    def copy(self, source, target, step, ctx):
        pltpu.make_async_remote_copy(
            src_ref=source,
            dst_ref=target,
            send_sem=self.sems.at[2 * step],
            recv_sem=self.sems.at[2 * step + 1],
            device_id={"ctx": ctx},
            device_id_type=MESH,
        ).start()

    def exchange(self):
        mine = self.gather.at[self.z]
        each_peer(
            self.Z,
            self.z,
            lambda peer: self.copy(self.piece(self.send, peer), mine, 0, self.x * self.Z + peer),
        )
        mine[...] = self.piece(self.send, self.z)[...]

    def total(self):
        rows, x = self.rows, self.x
        wait_for(self.gather.at[pl.ds(0, self.Z - 1)], self.sems.at[1])
        decay = jnp.exp(jnp.full((rows, HEAD), -float(TOK) * self.rate(), F32))
        state = jnp.zeros((rows, HEAD), F32)
        for place in self.order():
            self.pre[place] = state
            state = decay * state + self.gather[place].astype(F32)
        self.totals[x] = state
        mine = self.totals.at[x]
        each_peer(X, x, lambda peer: self.copy(mine, mine, 1, peer * self.Z + self.z))

    def finish(self):
        rows, x = self.rows, self.x
        wait_for(self.totals.at[pl.ds(0, X - 1)], self.sems.at[3])
        rate = self.rate()
        far = jnp.zeros((rows, HEAD), F32)
        for other in range(X):
            steps = (other - x - 1) if self.backward else (x - other - 1)
            reach = jnp.maximum(steps, 0).astype(F32) * (float(TOK) * self.Z)
            weight = jnp.exp(jnp.full((rows, HEAD), -reach * rate, F32))
            far = far + jnp.where(steps >= 0, weight * self.totals[other], 0.0)
        decay = jnp.exp(jnp.full((rows, HEAD), -float(TOK) * rate, F32))
        for place in self.order():
            self.back[place] = (self.pre[place] + far).astype(BF16)
            far = far * decay
        mine = self.piece(self.result, self.z)
        each_peer(
            self.Z,
            self.z,
            lambda peer: self.copy(self.back.at[peer], mine, 2, x * self.Z + peer),
        )
        mine[...] = self.back[self.z]

    def arrived(self):
        wait_for(self.back.at[pl.ds(0, self.Z - 1)], self.sems.at[5])

    def close(self):
        wait_for(self.gather.at[pl.ds(0, self.Z - 1)], self.sems.at[0])
        wait_for(self.totals.at[pl.ds(0, X - 1)], self.sems.at[2])
        wait_for(self.back.at[pl.ds(0, self.Z - 1)], self.sems.at[4])


def kernel(
    Z,
    DP,
    rate_hbm,
    gain_hbm,
    q_hbm,
    k_hbm,
    v_hbm,
    cot_hbm,
    k,
    v,
    normed,
    gq,
    gk_part,
    gv_part,
    rest_weight,
    later_out,
    gg_ref,
    rate_ref,
    gain_ref,
    q,
    cot,
    grad,
    weighted,
    probs,
    dscore,
    mask,
    down_base,
    up_base,
    attn,
    norm_parts,
    gain_z,
    gain_x,
    term,
    term_x,
    term_z,
    *rest,
):
    forward_refs, backward_refs = rest[0:7], rest[7:14]
    load_sems, small_sems = rest[14:]
    ctx, d = lax.axis_index("ctx"), lax.axis_index("dp")
    x, z = ctx // Z, lax.rem(ctx, Z)
    channels = DP * WIDE
    share = WIDE // (X * Z)

    barrier = pltpu.get_barrier_semaphore()

    def greet_row(peer):
        pl.semaphore_signal(
            barrier, inc=1, device_id={"ctx": x * Z + peer}, device_id_type=MESH
        )

    def greet_rows(peer):
        pl.semaphore_signal(
            barrier, inc=1, device_id={"ctx": peer * Z + z}, device_id_type=MESH
        )

    def greet_dp(peer):
        pl.semaphore_signal(barrier, inc=1, device_id={"dp": peer}, device_id_type=MESH)

    each_peer(Z, z, greet_row)
    each_peer(X, x, greet_rows)
    each_peer(DP, d, greet_dp)

    sources = ((k_hbm, k), (v_hbm, v), (q_hbm, q), (cot_hbm, cot))
    small_loads = [
        pltpu.make_async_copy(rate_hbm, rate_ref, load_sems.at[4]),
        pltpu.make_async_copy(gain_hbm, gain_ref, load_sems.at[5]),
    ]
    for load in small_loads:
        load.start()
    for i, (source, target) in enumerate(sources):
        for b in range(BLOCKS):
            part = pl.ds(b * SUB, SUB)
            pltpu.make_async_copy(source.at[part], target.at[part], load_sems.at[i]).start()

    def loaded(i):
        wait_for(sources[i][1], load_sems.at[i])

    place = (x, z, Z)
    ahead = Scan(place, rate_ref, False, forward_refs)
    behind = Scan(place, rate_ref, True, backward_refs)
    incoming, later = ahead.result, behind.result

    def lanes(h):
        return slice(h * HEAD, (h + 1) * HEAD)

    def rows_of(b):
        return slice(b * SUB, (b + 1) * SUB)

    def scaled(h, count):
        return jnp.exp(jnp.full((1, HEAD), -float(count) * rate_ref[h], F32))

    row_index = lax.broadcasted_iota(jnp.int32, (SUB, HEAD), 0).astype(F32)

    def make_up(h):
        up_base[h] = jnp.exp(-rate_ref[h] * (SUB - 1.0 - row_index))

    def make_down(h):
        down_base[h] = jnp.exp(-rate_ref[h] * row_index)

    def up(h, b, extra=0):
        return up_base[h] * scaled(h, SUB * (BLOCKS - 1 - b) + extra)

    def down(h, b, extra=0):
        return down_base[h] * scaled(h, SUB * b + extra)

    def make_mask(h):
        t = lax.broadcasted_iota(jnp.int32, (HALF, HALF), 0)
        i = lax.broadcasted_iota(jnp.int32, (HALF, HALF), 1)
        offset = (t - i).astype(F32)
        near = jnp.exp(-rate_ref[h] * jnp.maximum(offset, 0.0))
        mask[h, 0] = jnp.where(t >= i, near, 0.0)
        mask[h, 1] = jnp.exp(-rate_ref[h] * (offset + float(HALF)))

    def block_state(h):
        weighted_k = jnp.concatenate(
            [
                (k[rows_of(b), lanes(h)].astype(F32) * up(h, b)).astype(BF16)
                for b in range(BLOCKS)
            ],
            axis=0,
        )
        state = dot(weighted_k, v[:, lanes(h)], 0, 0)
        ahead.send[pl.ds(h * HEAD, HEAD)] = state.astype(BF16)

    def masked(h, left, right, out):
        for tb in range(2):
            rows = slice(tb * HALF, (tb + 1) * HALF)
            for ib in range(tb + 1):
                cols = slice(ib * HALF, (ib + 1) * HALF)
                score = dot(left[rows, lanes(h)], right[cols, lanes(h)], 1, 1)
                out[h, rows, cols] = (score * mask[h, tb - ib]).astype(BF16)

    def below(table, h, right):
        return (
            dot(table[h, 0:HALF, 0:HALF], right[0:HALF, lanes(h)], 1, 0),
            dot(table[h, HALF:TOK, :], right[:, lanes(h)], 1, 0),
        )

    def above(table, h, right):
        return (
            dot(table[h, :, 0:HALF], right[:, lanes(h)], 0, 0),
            dot(table[h, HALF:TOK, HALF:TOK], right[HALF:TOK, lanes(h)], 0, 0),
        )

    def local_part(h):
        make_mask(h)
        masked(h, q, k, probs)
        first, second = below(probs, h, v)
        attn[0:HALF, lanes(h)] = first
        attn[HALF:TOK, lanes(h)] = second

    def weigh_queries(h):
        make_down(h)
        for b in range(BLOCKS):
            weighted[rows_of(b), lanes(h)] = (
                q[rows_of(b), lanes(h)].astype(F32) * down(h, b)
            ).astype(BF16)
            rest_weight[h, rows_of(b)] = up(h, b, 1)

    def add_remote(h):
        remote = dot(q[:, lanes(h)], incoming[pl.ds(h * HEAD, HEAD)], 1, 0)
        for b in range(BLOCKS):
            attn[rows_of(b), lanes(h)] += down(h, b, 1) * remote[rows_of(b)]

    def send_row(source, target, kind, peer_ctx):
        pltpu.make_async_remote_copy(
            src_ref=source,
            dst_ref=target,
            send_sem=small_sems.at[kind],
            recv_sem=small_sems.at[kind + 1],
            device_id={"ctx": peer_ctx},
            device_id_type=MESH,
        ).start()

    lane = lax.broadcasted_iota(jnp.int32, (1, HEAD), 1)

    def gather_gain():
        own = jnp.zeros((1, HEAD), F32)
        for n in range(share):
            own = jnp.where(lane == z * share + n, gain_ref[n], own)
        gain_z[z] = own
        each_peer(Z, z, lambda peer: send_row(gain_z.at[z], gain_z.at[z], 0, x * Z + peer))

    def spread_gain():
        wait_for(gain_z.at[pl.ds(0, Z - 1)], small_sems.at[1])
        whole = gain_z[0]
        for n in range(1, Z):
            whole = whole + gain_z[n]
        gain_x[x] = whole
        each_peer(X, x, lambda peer: send_row(gain_x.at[x], gain_x.at[x], 2, peer * Z + z))

    def gain_arrived():
        wait_for(gain_x.at[pl.ds(0, X - 1)], small_sems.at[3])

    small_loads[0].wait()
    for h in range(LOCAL):
        make_up(h)
    loaded(0)
    loaded(1)
    for h in range(LOCAL):
        block_state(h)
    small_loads[1].wait()
    pl.semaphore_wait(barrier, (Z - 1) + (X - 1) + (DP - 1))
    ahead.exchange()
    gather_gain()
    loaded(2)
    for h in range(LOCAL):
        local_part(h)
    for h in range(LOCAL):
        weigh_queries(h)
    loaded(3)
    ahead.total()
    spread_gain()
    ahead.finish()
    gain_arrived()
    ahead.arrived()
    for h in range(LOCAL):
        add_remote(h)

    ones = jnp.ones((8, HEAD), F32)
    row8 = lax.broadcasted_iota(jnp.int32, (8, HEAD), 0)
    sums = jnp.zeros((8, HEAD), F32)
    for b in range(BLOCKS):
        square = jnp.zeros((SUB, HEAD), F32)
        cross = jnp.zeros((SUB, HEAD), F32)
        for h in range(LOCAL):
            a = attn[rows_of(b), lanes(h)]
            square = square + a * a
            cross = cross + cot[rows_of(b), lanes(h)].astype(F32) * gain_x[h] * a
        sums = jnp.where(row8 == b, dot(ones, square, 1, 1, HIGH), sums)
        sums = jnp.where(row8 == b + BLOCKS, dot(ones, cross, 1, 1, HIGH), sums)
    norm_parts[d] = sums

    def send_norm(peer):
        pltpu.make_async_remote_copy(
            src_ref=norm_parts.at[d],
            dst_ref=norm_parts.at[d],
            send_sem=small_sems.at[4],
            recv_sem=small_sems.at[5],
            device_id={"dp": peer},
            device_id_type=MESH,
        ).start()

    each_peer(DP, d, send_norm)
    wait_for(norm_parts.at[pl.ds(0, DP - 1)], small_sems.at[5])
    whole = norm_parts[0]
    for n in range(1, DP):
        whole = whole + norm_parts[n]
    inverse_rows = lax.rsqrt(whole[0:BLOCKS] / channels + eps_norm)
    cross_rows = inverse_rows * inverse_rows * inverse_rows * whole[BLOCKS : 2 * BLOCKS] / channels

    def column(rows, b):
        return jnp.broadcast_to(rows[b : b + 1], (SUB, HEAD)).T

    inverse = [column(inverse_rows, b) for b in range(BLOCKS)]
    cross_part = [column(cross_rows, b) for b in range(BLOCKS)]

    def back_state(h):
        for b in range(BLOCKS):
            at = (rows_of(b), lanes(h))
            grad[at] = (
                cot[at].astype(F32) * gain_x[h] * inverse[b] - attn[at] * cross_part[b]
            ).astype(BF16)
        state = dot(weighted[:, lanes(h)], grad[:, lanes(h)], 0, 0)
        behind.send[pl.ds(h * HEAD, HEAD)] = state.astype(BF16)

    def norm_out(h):
        total = jnp.zeros((1, HEAD), F32)
        for b in range(BLOCKS):
            at = (rows_of(b), lanes(h))
            scaled_attn = attn[at] * inverse[b]
            normed[at] = (scaled_attn * gain_x[h]).astype(BF16)
            total = total + jnp.sum(cot[at].astype(F32) * scaled_attn, axis=0, keepdims=True)
        term[h] = total

    def spread_term():
        each_peer(X, x, lambda peer: send_row(term.at[peer], term_x.at[x], 6, peer * Z + z))
        term_x[x] = term[x]

    def gather_term():
        wait_for(term_x.at[pl.ds(0, X - 1)], small_sems.at[7])
        whole = term_x[0]
        for n in range(1, X):
            whole = whole + term_x[n]
        term_z[z] = whole
        each_peer(Z, z, lambda peer: send_row(term_z.at[z], term_z.at[z], 8, x * Z + peer))

    def finish_term():
        wait_for(term_z.at[pl.ds(0, Z - 1)], small_sems.at[9])
        whole = term_z[0]
        for n in range(1, Z):
            whole = whole + term_z[n]
        source = lax.broadcasted_iota(jnp.int32, (HEAD, HEAD), 0)
        target = lax.broadcasted_iota(jnp.int32, (HEAD, HEAD), 1)
        pick = (source == target + z * share).astype(F32)
        mine = dot(jnp.broadcast_to(whole, (8, HEAD)), pick, 1, 0, HIGH)
        gg_ref[...] = mine[0:1, 0:share]

    def gradient_part(h):
        masked(h, grad, v, dscore)
        near = below(dscore, h, k)
        far = dot(grad[:, lanes(h)], incoming[pl.ds(h * HEAD, HEAD)], 1, 1)
        for b in range(BLOCKS):
            half, inner = divmod(b * SUB, HALF)
            gq[rows_of(b), lanes(h)] = (
                near[half][inner : inner + SUB] + down(h, b, 1) * far[rows_of(b)]
            ).astype(BF16)
        first, second = above(dscore, h, q)
        gk_part[0:HALF, lanes(h)] = first
        gk_part[HALF:TOK, lanes(h)] = second
        first, second = above(probs, h, grad)
        gv_part[0:HALF, lanes(h)] = first
        gv_part[HALF:TOK, lanes(h)] = second

    for h in range(LOCAL):
        back_state(h)
    behind.exchange()
    for h in range(LOCAL):
        norm_out(h)
    spread_term()
    gradient_part(0)
    gradient_part(1)
    gather_term()
    gradient_part(2)
    gradient_part(3)
    behind.total()
    behind.finish()
    finish_term()
    behind.arrived()
    later_out[...] = later[...]

    ahead.close()
    behind.close()
    wait_for(gain_z.at[pl.ds(0, Z - 1)], small_sems.at[0])
    wait_for(gain_x.at[pl.ds(0, X - 1)], small_sems.at[2])
    wait_for(norm_parts.at[pl.ds(0, DP - 1)], small_sems.at[4])
    wait_for(term_x.at[pl.ds(0, X - 1)], small_sems.at[6])
    wait_for(term_z.at[pl.ds(0, Z - 1)], small_sems.at[8])


def writer(
    k,
    v,
    normed,
    gq,
    gk_part,
    gv_part,
    rest_weight,
    later,
    gain_sum,
    normed_hbm,
    gq_hbm,
    gk_hbm,
    gv_hbm,
    gg_hbm,
    gk,
    gv,
    sems,
):
    pltpu.make_async_copy(gain_sum, gg_hbm, sems.at[4]).start()

    def write(i, source, target, b):
        part = pl.ds(b * SUB, SUB)
        pltpu.make_async_copy(source.at[part], target.at[part], sems.at[i]).start()

    for b in range(BLOCKS):
        write(0, normed, normed_hbm, b)
        write(1, gq, gq_hbm, b)
    for b in range(BLOCKS):
        rows = slice(b * SUB, (b + 1) * SUB)
        for h in range(LOCAL):
            at = (rows, slice(h * HEAD, (h + 1) * HEAD))
            state = later[pl.ds(h * HEAD, HEAD)]
            weight = rest_weight[h, rows]
            gk[at] = (gk_part[at] + weight * dot(v[at], state, 1, 1)).astype(BF16)
            gv[at] = (gv_part[at] + weight * dot(k[at], state, 1, 0)).astype(BF16)
        write(2, gk, gk_hbm, b)
        write(3, gv, gv_hbm, b)
    for i, whole in enumerate((normed, gq, gk, gv, gain_sum)):
        wait_for(whole, sems.at[i])


def per_device(Z, DP, queries, keys, values, cotangent, log_decay, gain):
    rows = WIDE // Z
    share = gain.shape[0]
    tokens = pltpu.VMEM((TOK, WIDE), BF16)
    square = pltpu.VMEM((LOCAL, TOK, TOK), BF16)
    scan = [
        pltpu.VMEM((WIDE, HEAD), BF16),
        pltpu.VMEM((Z, rows, HEAD), BF16),
        pltpu.VMEM((Z, rows, HEAD), F32),
        pltpu.VMEM((X, rows, HEAD), F32),
        pltpu.VMEM((Z, rows, HEAD), BF16),
        pltpu.VMEM((WIDE, HEAD), BF16),
        pltpu.SemaphoreType.DMA((6,)),
    ]
    half, full = jax.ShapeDtypeStruct((TOK, WIDE), BF16), jax.ShapeDtypeStruct((TOK, WIDE), F32)
    hbm = pl.BlockSpec(memory_space=pltpu.HBM)
    vmem = pl.BlockSpec(memory_space=pltpu.VMEM)
    inputs = [
        pltpu.with_memory_space_constraint(array, pltpu.HBM)
        for array in (log_decay, gain, queries, keys, values, cotangent)
    ]
    held = pl.pallas_call(
        functools.partial(kernel, Z, DP),
        out_shape=[
            half,
            half,
            half,
            half,
            full,
            full,
            jax.ShapeDtypeStruct((LOCAL, TOK, HEAD), F32),
            jax.ShapeDtypeStruct((WIDE, HEAD), BF16),
            jax.ShapeDtypeStruct((1, share), F32),
        ],
        in_specs=[hbm] * 6,
        out_specs=[vmem] * 9,
        scratch_shapes=[
            pltpu.SMEM((LOCAL,), F32),
            pltpu.SMEM((share,), F32),
            tokens,
            tokens,
            tokens,
            tokens,
            square,
            square,
            pltpu.VMEM((LOCAL, 2, HALF, HALF), F32),
            pltpu.VMEM((LOCAL, SUB, HEAD), F32),
            pltpu.VMEM((LOCAL, SUB, HEAD), F32),
            pltpu.VMEM((TOK, WIDE), F32),
            pltpu.VMEM((DP, 8, HEAD), F32),
            pltpu.VMEM((Z, 1, HEAD), F32),
            pltpu.VMEM((X, 1, HEAD), F32),
            pltpu.VMEM((LOCAL, 1, HEAD), F32),
            pltpu.VMEM((X, 1, HEAD), F32),
            pltpu.VMEM((Z, 1, HEAD), F32),
        ]
        + scan
        + scan
        + [pltpu.SemaphoreType.DMA((6,)), pltpu.SemaphoreType.DMA((10,))],
        compiler_params=pltpu.CompilerParams(
            collective_id=0, has_side_effects=True, vmem_limit_bytes=40 * 1024 * 1024
        ),
        cost_estimate=pl.CostEstimate(
            flops=2_000_000_000, bytes_accessed=4_200_000, transcendentals=700_000
        ),
    )(*inputs)
    normed, gq, gk, gv, gg = pl.pallas_call(
        writer,
        out_shape=[half, half, half, half, jax.ShapeDtypeStruct((1, share), F32)],
        in_specs=[vmem] * 9,
        out_specs=[hbm] * 5,
        scratch_shapes=[tokens, tokens, pltpu.SemaphoreType.DMA((5,))],
        compiler_params=pltpu.CompilerParams(vmem_limit_bytes=24 * 1024 * 1024),
        cost_estimate=pl.CostEstimate(
            flops=300_000_000, bytes_accessed=2_200_000, transcendentals=0
        ),
    )(*held)
    return normed, gq, gk, gv, gg.reshape(share)


def solution(mesh):
    both = P("ctx", "dp")
    return jax.shard_map(
        functools.partial(per_device, mesh.shape["ctx"] // X, mesh.shape["dp"]),
        mesh=mesh,
        in_specs=(both, both, both, both, P("dp"), P(("dp", "ctx"))),
        out_specs=(both, both, both, both, P(("dp", "ctx"))),
        check_vma=False,
    )
```

```python
import functools

import jax
import jax.numpy as jnp
from jax import lax
from jax.experimental import pallas as pl
from jax.experimental.pallas import tpu as pltpu
from jax.sharding import PartitionSpec as P

HEAD = 128
LOCAL = 4
TOK = 512
WIDE = LOCAL * HEAD
SUB = 128
BLOCKS = TOK // SUB
HALF = 256
X = 4
WINDOW = 4
PIECE = HEAD // WINDOW
NEAR = (0, 1, -1, -2)

eps_norm = 1e-06
F32, BF16 = jnp.float32, jnp.bfloat16
MESH = pl.DeviceIdType.MESH
HIGH = lax.Precision.HIGHEST


def dot(a, b, over_a, over_b, precision=None):
    return lax.dot_general(
        a, b, (((over_a,), (over_b,)), ((), ())), precision=precision, preferred_element_type=F32
    )


def each_peer(count, me, body):
    for i in range(count - 1):
        offset = count // 2 + ((i + 1) // 2) * (1 - 2 * (i % 2))
        body(lax.rem(me + offset, count))


def near_places(steps):
    pairs = [(a, b) for a in range(X) for b in steps if (a, b) != (0, 0)]
    return sorted(pairs, key=lambda p: -(min(p[0], X - p[0]) + abs(p[1])))


def wait_for(ref, sem):
    pltpu.make_async_copy(ref, ref, sem).wait()


class Scan:
    def __init__(self, place, rate_ref, backward, refs):
        self.x, self.z, self.Z = place
        self.rate_ref = rate_ref
        self.backward = backward
        self.send, self.gather, self.inner, self.own, self.out, self.far, self.outer = refs[:7]
        self.back, self.result, self.sems = refs[7:]
        self.first = lax.rem(self.z + self.Z - 2, self.Z)
        self.shift = [(self.first + q) // self.Z for q in range(WINDOW)]
        self.ring = range(WINDOW, self.Z, WINDOW)

    def clear(self):
        zero = jnp.zeros((PIECE, HEAD), F32)
        for q in range(WINDOW):
            self.gather[q, 0] = zero.astype(BF16)
            self.gather[q, X + 1] = zero.astype(BF16)
        for j in range(len(self.ring)):
            for i in (0, 1, X + 1, X + 2):
                self.far[j, i] = zero.astype(BF16)
        self.own[0] = zero
        self.own[X + 2] = zero

    def piece(self, ref, x, z):
        start = (x * WINDOW + lax.rem(z, WINDOW)) * PIECE
        return ref.at[pl.ds(pl.multiple_of(start, PIECE), PIECE)]

    def decay(self, blocks):
        return jnp.exp(jnp.full((1, HEAD), -float(TOK * blocks) * self.rate_ref[self.x], F32))

    def copy(self, source, target, step, x, z):
        pltpu.make_async_remote_copy(
            src_ref=source,
            dst_ref=target,
            send_sem=self.sems.at[2 * step],
            recv_sem=self.sems.at[2 * step + 1],
            device_id={"ctx": x * self.Z + z},
            device_id_type=MESH,
        ).start()

    def at(self, a, b):
        return lax.rem(self.x + a, X), lax.rem(self.z + b + self.Z, self.Z)

    def wait_near(self, sem):
        wait_for(self.gather.at[pl.ds(0, 3), pl.ds(0, 5)], self.sems.at[sem])

    def wait_far(self, sem):
        wait_for(self.far.at[:, pl.ds(0, X)], self.sems.at[sem])

    def exchange(self):
        for a in (2, 1, 3, 0):
            self.exchange_with(a)
        self.keep()

    def exchange_with(self, a):
        for b in (2, 1, -1, 0):
            if (a, b) != (0, 0):
                x, z = self.at(a, b)
                self.copy(self.piece(self.send, x, z), self.gather.at[2 - b, self.x + 1], 0, x, z)

    def keep(self):
        self.gather[2, self.x + 1] = self.piece(self.send, self.x, self.z)[...]

    def total(self):
        decay, row_decay = self.decay(1), self.decay(self.Z)
        instances, slots = range(X + 1), range(WINDOW)
        if self.backward:
            instances, slots = instances[::-1], slots[::-1]
        self.wait_near(1)
        running = jnp.zeros((PIECE, HEAD), F32)
        for i in instances:
            state = jnp.zeros((PIECE, HEAD), F32)
            for q in slots:
                self.inner[i, q] = state
                state = decay * state + self.gather[q, i + self.shift[q]].astype(F32)
            running = row_decay * running + state
            self.own[i + 1] = running
            self.out[i] = running.astype(BF16)
        for j, distance in sorted(enumerate(self.ring), key=lambda p: -min(p[1], self.Z - p[1])):
            x, z = self.at(0, distance)
            start = 1 if self.backward else jnp.where(self.first + distance < self.Z, 1, 0)
            self.copy(self.out.at[pl.ds(start, X)], self.far.at[j, pl.ds(start + 1, X)], 1, x, z)

    def finish(self):
        gaps, offsets = [], []
        for distance in self.ring:
            if self.backward:
                gaps.append(self.decay(self.Z - distance - WINDOW))
                offsets.append(1 + jnp.where(self.first < distance, 0, 1))
            else:
                gaps.append(self.decay(distance - WINDOW))
                offsets.append(1 - jnp.where(self.first >= distance, 0, 1))
        own_gap = self.decay(self.Z - WINDOW)
        reach = [self.decay(WINDOW - 1 - q if self.backward else q) for q in range(WINDOW)]
        self.wait_far(3)
        for i in range(X + 1):
            total = own_gap * self.own[i + 2 if self.backward else i]
            for j, (gap, offset) in enumerate(zip(gaps, offsets)):
                total = total + gap * self.far[j, i + offset].astype(F32)
            self.outer[i] = total
        for x in range(X):
            for q in range(WINDOW):
                i = x + 1 - self.shift[q]
                self.back[x, q] = (reach[q] * self.outer[i] + self.inner[i, q]).astype(BF16)
        mine = self.piece(self.result, self.x, self.z)
        for a, b in near_places((-2, -1, 0, 1)):
            x, z = self.at(a, b)
            self.copy(self.back.at[x, b + 2], mine, 2, x, z)
        mine[...] = self.back[self.x, 2]

    def arrived(self):
        self.wait_near(5)

    def close(self):
        self.wait_near(0)
        self.wait_far(2)
        self.wait_near(4)


def kernel(
    Z,
    DP,
    rate_hbm,
    gain_hbm,
    q_hbm,
    k_hbm,
    v_hbm,
    cot_hbm,
    k,
    v,
    normed,
    gq,
    gk_part,
    gv_part,
    rest_weight,
    later_out,
    gg_ref,
    rate_ref,
    gain_ref,
    q,
    cot,
    grad,
    weighted,
    probs,
    dscore,
    mask,
    down_base,
    up_base,
    attn,
    cot_gain,
    norm_parts,
    gain_near,
    gain_far,
    gain_x,
    term,
    term_x,
    term_near,
    term_far,
    *rest,
):
    forward_refs, backward_refs = rest[0:10], rest[10:20]
    load_sems, small_sems, relay = rest[20:]
    ctx, d = lax.axis_index("ctx"), lax.axis_index("dp")
    x, z = ctx // Z, lax.rem(ctx, Z)
    channels = DP * WIDE
    share = WIDE // (X * Z)

    place = (x, z, Z)
    ahead = Scan(place, rate_ref, False, forward_refs)
    behind = Scan(place, rate_ref, True, backward_refs)
    incoming, later = ahead.result, behind.result
    ahead.clear()
    behind.clear()

    barrier = pltpu.get_barrier_semaphore()

    def ring(b):
        return lax.rem(z + b + Z, Z)

    far_steps = range(WINDOW, Z, WINDOW)
    near = near_places((2, 1, 0, -1, -2))
    for a, b in near:
        target = lax.rem(x + a, X) * Z + ring(b)
        pl.semaphore_signal(barrier, inc=1, device_id={"ctx": target}, device_id_type=MESH)

    def tell(n, steps):
        for b in (steps, -steps):
            pl.semaphore_signal(
                relay.at[n], inc=1, device_id={"ctx": x * Z + ring(b)}, device_id_type=MESH
            )

    def told(n):
        pl.semaphore_wait(relay.at[n], 2)

    def greet_dp(peer):
        pl.semaphore_signal(barrier, inc=1, device_id={"dp": peer}, device_id_type=MESH)

    each_peer(DP, d, greet_dp)

    sources = ((k_hbm, k), (v_hbm, v), (q_hbm, q), (cot_hbm, cot))
    small_loads = [
        pltpu.make_async_copy(rate_hbm, rate_ref, load_sems.at[4]),
        pltpu.make_async_copy(gain_hbm, gain_ref, load_sems.at[5]),
    ]
    for load in small_loads:
        load.start()
    for i, (source, target) in enumerate(sources):
        for b in range(BLOCKS):
            part = pl.ds(b * SUB, SUB)
            pltpu.make_async_copy(source.at[part], target.at[part], load_sems.at[i]).start()

    def loaded(i):
        wait_for(sources[i][1], load_sems.at[i])

    def lanes(h):
        return pl.ds(h * HEAD if isinstance(h, int) else pl.multiple_of(h * HEAD, HEAD), HEAD)

    def rows_of(b):
        return slice(b * SUB, (b + 1) * SUB)

    def scaled(h, count):
        return jnp.exp(jnp.full((1, HEAD), -float(count) * rate_ref[h], F32))

    row_index = lax.broadcasted_iota(jnp.int32, (SUB, HEAD), 0).astype(F32)

    def make_up(h):
        up_base[h] = jnp.exp(-rate_ref[h] * (SUB - 1.0 - row_index))

    def make_down(h):
        down_base[h] = jnp.exp(-rate_ref[h] * row_index)

    def up(h, b, extra=0):
        return up_base[h] * scaled(h, SUB * (BLOCKS - 1 - b) + extra)

    def down(h, b, extra=0):
        return down_base[h] * scaled(h, SUB * b + extra)

    def make_mask(h):
        t = lax.broadcasted_iota(jnp.int32, (HALF, HALF), 0)
        i = lax.broadcasted_iota(jnp.int32, (HALF, HALF), 1)
        offset = (t - i).astype(F32)
        near = jnp.exp(-rate_ref[h] * jnp.maximum(offset, 0.0))
        mask[h, 0] = jnp.where(t >= i, near, 0.0)
        mask[h, 1] = jnp.exp(-rate_ref[h] * (offset + float(HALF)))

    def block_state(h):
        weighted_k = jnp.concatenate(
            [
                (k[rows_of(b), lanes(h)].astype(F32) * up(h, b)).astype(BF16)
                for b in range(BLOCKS)
            ],
            axis=0,
        )
        state = dot(weighted_k, v[:, lanes(h)], 0, 0)
        ahead.send[pl.ds(h * HEAD, HEAD)] = state.astype(BF16)

    def masked(h, left, right, out):
        for tb in range(2):
            rows = slice(tb * HALF, (tb + 1) * HALF)
            for ib in range(tb + 1):
                cols = slice(ib * HALF, (ib + 1) * HALF)
                score = dot(left[rows, lanes(h)], right[cols, lanes(h)], 1, 1)
                out[h, rows, cols] = (score * mask[h, tb - ib]).astype(BF16)

    def below(table, h, right):
        return (
            dot(table[h, 0:HALF, 0:HALF], right[0:HALF, lanes(h)], 1, 0),
            dot(table[h, HALF:TOK, :], right[:, lanes(h)], 1, 0),
        )

    def above(table, h, right):
        return (
            dot(table[h, :, 0:HALF], right[:, lanes(h)], 0, 0),
            dot(table[h, HALF:TOK, HALF:TOK], right[HALF:TOK, lanes(h)], 0, 0),
        )

    def local_part(h):
        make_mask(h)
        masked(h, q, k, probs)
        first, second = below(probs, h, v)
        attn[0:HALF, lanes(h)] = first
        attn[HALF:TOK, lanes(h)] = second

    def weigh_queries(h):
        make_down(h)
        for b in range(BLOCKS):
            weighted_q = q[rows_of(b), lanes(h)].astype(F32) * down(h, b)
            weighted[h, :, rows_of(b)] = weighted_q.T.astype(BF16)
            rest_weight[h, rows_of(b)] = up(h, b, 1)

    def send_row(source, target, kind, peer_ctx):
        pltpu.make_async_remote_copy(
            src_ref=source,
            dst_ref=target,
            send_sem=small_sems.at[kind],
            recv_sem=small_sems.at[kind + 1],
            device_id={"ctx": peer_ctx},
            device_id_type=MESH,
        ).start()

    lane = lax.broadcasted_iota(jnp.int32, (1, HEAD), 1)

    def sum_of(ref):
        total = ref[0]
        for n in range(1, ref.shape[0]):
            total = total + ref[n]
        return total

    def sum_near(ref, kind):
        for n in range(1, WINDOW):
            send_row(ref.at[0], ref.at[n], kind, x * Z + ring(NEAR[n]))

    def sum_far(ref, kind):
        for n, b in enumerate(far_steps):
            send_row(ref.at[0], ref.at[n + 1], kind, x * Z + ring(b))

    def rows_arrived(ref, sem):
        wait_for(ref.at[pl.ds(0, ref.shape[0] - 1)], small_sems.at[sem])

    def gain_first():
        own = jnp.zeros((1, HEAD), F32)
        for n in range(share):
            own = jnp.where(lane == z * share + n, gain_ref[n], own)
        gain_near[0] = own
        sum_near(gain_near, 0)

    def gain_second():
        rows_arrived(gain_near, 1)
        gain_far[0] = sum_of(gain_near)
        sum_far(gain_far, 2)

    def gain_third():
        rows_arrived(gain_far, 3)
        gain_x[x] = sum_of(gain_far)
        each_peer(X, x, lambda peer: send_row(gain_x.at[x], gain_x.at[x], 4, peer * Z + z))

    small_loads[0].wait()
    for h in range(LOCAL):
        make_up(h)
    loaded(0)
    loaded(1)
    for h in range(LOCAL):
        block_state(h)
    small_loads[1].wait()
    pl.semaphore_wait(barrier, len(near) + DP - 1)
    tell(0, 2)
    gain_first()
    ahead.exchange()
    loaded(2)
    local_part(0)
    told(0)
    tell(1, 4)
    local_part(1)
    told(1)
    gain_second()
    ahead.total()
    local_part(2)
    local_part(3)
    for h in range(LOCAL):
        weigh_queries(h)
    loaded(3)
    ahead.finish()
    gain_third()
    rows_arrived(gain_x, 5)
    for h in range(LOCAL):
        for b in range(BLOCKS):
            at = (rows_of(b), lanes(h))
            cot_gain[at] = cot[at].astype(F32) * gain_x[h]
    factors = [[scaled(h, SUB * b + 1) for b in range(BLOCKS)] for h in range(LOCAL)]
    ahead.arrived()

    remote = [
        dot(q[:, lanes(h)], incoming[pl.ds(h * HEAD, HEAD)], 1, 0) for h in range(LOCAL)
    ]
    row8 = lax.broadcasted_iota(jnp.int32, (8, HEAD), 0)
    sums = jnp.zeros((8, HEAD), F32)
    for b in range(BLOCKS):
        square = jnp.zeros((SUB, HEAD), F32)
        cross = jnp.zeros((SUB, HEAD), F32)
        for h in range(LOCAL):
            at = (rows_of(b), lanes(h))
            a = attn[at] + down_base[h] * factors[h][b] * remote[h][rows_of(b)]
            attn[at] = a
            square = square + a * a
            cross = cross + cot_gain[at] * a
        sums = jnp.where(row8 == b, jnp.sum(square.T, axis=0, keepdims=True), sums)
        sums = jnp.where(row8 == b + BLOCKS, jnp.sum(cross.T, axis=0, keepdims=True), sums)
    norm_parts[d] = sums

    def send_norm(peer):
        pltpu.make_async_remote_copy(
            src_ref=norm_parts.at[d],
            dst_ref=norm_parts.at[d],
            send_sem=small_sems.at[12],
            recv_sem=small_sems.at[13],
            device_id={"dp": peer},
            device_id_type=MESH,
        ).start()

    each_peer(DP, d, send_norm)
    rows_arrived(norm_parts, 13)
    whole = norm_parts[0]
    for n in range(1, DP):
        whole = whole + norm_parts[n]
    inverse_rows = lax.rsqrt(whole[0:BLOCKS] / channels + eps_norm)
    cross_rows = inverse_rows * inverse_rows * inverse_rows * whole[BLOCKS : 2 * BLOCKS] / channels

    def column(rows, b):
        return jnp.broadcast_to(rows[b : b + 1], (SUB, HEAD)).T

    inverse = [column(inverse_rows, b) for b in range(BLOCKS)]
    cross_part = [column(cross_rows, b) for b in range(BLOCKS)]

    def back_state(h):
        for b in range(BLOCKS):
            at = (rows_of(b), lanes(h))
            grad[at] = (
                cot_gain[at] * inverse[b] - attn[at] * cross_part[b]
            ).astype(BF16)
        state = dot(weighted[h], grad[:, lanes(h)], 1, 0)
        behind.send[pl.ds(pl.multiple_of(h * HEAD, HEAD), HEAD)] = state.astype(BF16)

    def norm_out(h):
        total = jnp.zeros((1, HEAD), F32)
        for b in range(BLOCKS):
            at = (rows_of(b), lanes(h))
            scaled_attn = attn[at] * inverse[b]
            normed[at] = (scaled_attn * gain_x[h]).astype(BF16)
            total = total + jnp.sum(cot[at].astype(F32) * scaled_attn, axis=0, keepdims=True)
        term[h] = total

    def spread_term():
        each_peer(X, x, lambda peer: send_row(term.at[peer], term_x.at[x], 6, peer * Z + z))
        term_x[x] = term[x]

    def term_second():
        rows_arrived(term_x, 7)
        term_near[0] = sum_of(term_x)
        sum_near(term_near, 8)

    def term_third():
        rows_arrived(term_near, 9)
        term_far[0] = sum_of(term_near)
        sum_far(term_far, 10)

    def finish_term():
        rows_arrived(term_far, 11)
        whole = sum_of(term_far)
        source = lax.broadcasted_iota(jnp.int32, (HEAD, HEAD), 0)
        target = lax.broadcasted_iota(jnp.int32, (HEAD, HEAD), 1)
        pick = (source == target + z * share).astype(F32)
        mine = dot(jnp.broadcast_to(whole, (8, HEAD)), pick, 1, 0, HIGH)
        gg_ref[...] = mine[0:1, 0:share]

    def gradient_part(h):
        masked(h, grad, v, dscore)
        near = below(dscore, h, k)
        far = dot(grad[:, lanes(h)], incoming[pl.ds(h * HEAD, HEAD)], 1, 1)
        for b in range(BLOCKS):
            half, inner = divmod(b * SUB, HALF)
            gq[rows_of(b), lanes(h)] = (
                near[half][inner : inner + SUB] + down(h, b, 1) * far[rows_of(b)]
            ).astype(BF16)
        first, second = above(dscore, h, q)
        gk_part[0:HALF, lanes(h)] = first
        gk_part[HALF:TOK, lanes(h)] = second
        first, second = above(probs, h, grad)
        gv_part[0:HALF, lanes(h)] = first
        gv_part[HALF:TOK, lanes(h)] = second

    for a in (2, 1, 3, 0):
        h = lax.rem(x + a, LOCAL)
        back_state(h)
        behind.exchange_with(a)
    behind.keep()
    for h in range(LOCAL):
        norm_out(h)
    spread_term()
    gradient_part(0)
    gradient_part(1)
    behind.total()
    term_second()
    gradient_part(2)
    gradient_part(3)
    term_third()
    behind.finish()
    finish_term()
    behind.arrived()
    later_out[...] = later[...]

    ahead.close()
    behind.close()
    rows_arrived(gain_near, 0)
    rows_arrived(gain_far, 2)
    rows_arrived(gain_x, 4)
    rows_arrived(term_x, 6)
    rows_arrived(term_near, 8)
    rows_arrived(term_far, 10)
    rows_arrived(norm_parts, 12)


def writer(
    k,
    v,
    normed,
    gq,
    gk_part,
    gv_part,
    rest_weight,
    later,
    gain_sum,
    normed_hbm,
    gq_hbm,
    gk_hbm,
    gv_hbm,
    gg_hbm,
    gk,
    gv,
    sems,
):
    pltpu.make_async_copy(gain_sum, gg_hbm, sems.at[4]).start()

    def write(i, source, target, b):
        part = pl.ds(b * SUB, SUB)
        pltpu.make_async_copy(source.at[part], target.at[part], sems.at[i]).start()

    for b in range(BLOCKS):
        write(0, normed, normed_hbm, b)
        write(1, gq, gq_hbm, b)
    for b in range(BLOCKS):
        rows = slice(b * SUB, (b + 1) * SUB)
        for h in range(LOCAL):
            at = (rows, slice(h * HEAD, (h + 1) * HEAD))
            state = later[pl.ds(h * HEAD, HEAD)]
            weight = rest_weight[h, rows]
            gk[at] = (gk_part[at] + weight * dot(v[at], state, 1, 1)).astype(BF16)
            gv[at] = (gv_part[at] + weight * dot(k[at], state, 1, 0)).astype(BF16)
        write(2, gk, gk_hbm, b)
        write(3, gv, gv_hbm, b)
    for i, whole in enumerate((normed, gq, gk, gv, gain_sum)):
        wait_for(whole, sems.at[i])


def per_device(Z, DP, queries, keys, values, cotangent, log_decay, gain):
    owners = Z // WINDOW
    share = gain.shape[0]
    tokens = pltpu.VMEM((TOK, WIDE), BF16)
    square = pltpu.VMEM((LOCAL, TOK, TOK), BF16)
    scan = [
        pltpu.VMEM((WIDE, HEAD), BF16),
        pltpu.VMEM((WINDOW, X + 2, PIECE, HEAD), BF16),
        pltpu.VMEM((X + 1, WINDOW, PIECE, HEAD), F32),
        pltpu.VMEM((X + 3, PIECE, HEAD), F32),
        pltpu.VMEM((X + 1, PIECE, HEAD), BF16),
        pltpu.VMEM((owners - 1, X + 3, PIECE, HEAD), BF16),
        pltpu.VMEM((X + 1, PIECE, HEAD), F32),
        pltpu.VMEM((X, WINDOW, PIECE, HEAD), BF16),
        pltpu.VMEM((WIDE, HEAD), BF16),
        pltpu.SemaphoreType.DMA((6,)),
    ]
    half, full = jax.ShapeDtypeStruct((TOK, WIDE), BF16), jax.ShapeDtypeStruct((TOK, WIDE), F32)
    hbm = pl.BlockSpec(memory_space=pltpu.HBM)
    vmem = pl.BlockSpec(memory_space=pltpu.VMEM)
    inputs = [
        pltpu.with_memory_space_constraint(array, pltpu.HBM)
        for array in (log_decay, gain, queries, keys, values, cotangent)
    ]
    held = pl.pallas_call(
        functools.partial(kernel, Z, DP),
        out_shape=[
            half,
            half,
            half,
            half,
            full,
            full,
            jax.ShapeDtypeStruct((LOCAL, TOK, HEAD), F32),
            jax.ShapeDtypeStruct((WIDE, HEAD), BF16),
            jax.ShapeDtypeStruct((1, share), F32),
        ],
        in_specs=[hbm] * 6,
        out_specs=[vmem] * 9,
        scratch_shapes=[
            pltpu.SMEM((LOCAL,), F32),
            pltpu.SMEM((share,), F32),
            tokens,
            tokens,
            tokens,
            pltpu.VMEM((LOCAL, HEAD, TOK), BF16),
            square,
            square,
            pltpu.VMEM((LOCAL, 2, HALF, HALF), F32),
            pltpu.VMEM((LOCAL, SUB, HEAD), F32),
            pltpu.VMEM((LOCAL, SUB, HEAD), F32),
            pltpu.VMEM((TOK, WIDE), F32),
            pltpu.VMEM((TOK, WIDE), F32),
            pltpu.VMEM((DP, 8, HEAD), F32),
            pltpu.VMEM((WINDOW, 1, HEAD), F32),
            pltpu.VMEM((owners, 1, HEAD), F32),
            pltpu.VMEM((X, 1, HEAD), F32),
            pltpu.VMEM((LOCAL, 1, HEAD), F32),
            pltpu.VMEM((X, 1, HEAD), F32),
            pltpu.VMEM((WINDOW, 1, HEAD), F32),
            pltpu.VMEM((owners, 1, HEAD), F32),
        ]
        + scan
        + scan
        + [pltpu.SemaphoreType.DMA((6,)), pltpu.SemaphoreType.DMA((14,)), pltpu.SemaphoreType.REGULAR((2,))],
        compiler_params=pltpu.CompilerParams(
            collective_id=0, has_side_effects=True, vmem_limit_bytes=40 * 1024 * 1024
        ),
        cost_estimate=pl.CostEstimate(
            flops=2_000_000_000, bytes_accessed=4_200_000, transcendentals=700_000
        ),
    )(*inputs)
    normed, gq, gk, gv, gg = pl.pallas_call(
        writer,
        out_shape=[half, half, half, half, jax.ShapeDtypeStruct((1, share), F32)],
        in_specs=[vmem] * 9,
        out_specs=[hbm] * 5,
        scratch_shapes=[tokens, tokens, pltpu.SemaphoreType.DMA((5,))],
        compiler_params=pltpu.CompilerParams(vmem_limit_bytes=24 * 1024 * 1024),
        cost_estimate=pl.CostEstimate(
            flops=300_000_000, bytes_accessed=2_200_000, transcendentals=0
        ),
    )(*held)
    return normed, gq, gk, gv, gg.reshape(share)


def solution(mesh):
    both = P("ctx", "dp")
    return jax.shard_map(
        functools.partial(per_device, mesh.shape["ctx"] // X, mesh.shape["dp"]),
        mesh=mesh,
        in_specs=(both, both, both, both, P("dp"), P(("dp", "ctx"))),
        out_specs=(both, both, both, both, P(("dp", "ctx"))),
        check_vma=False,
    )
```

```python
import functools

import jax
import jax.numpy as jnp
from jax import lax
from jax.experimental import pallas as pl
from jax.experimental.pallas import tpu as pltpu
from jax.sharding import PartitionSpec as P

HEAD = 128
LOCAL = 4
TOK = 512
WIDE = LOCAL * HEAD
SUB = 128
BLOCKS = TOK // SUB
HALF = 256
X = 4
WINDOW = 4
PIECE = HEAD // WINDOW
NEAR = (0, 1, -1, -2)

eps_norm = 1e-06
F32, BF16 = jnp.float32, jnp.bfloat16
MESH = pl.DeviceIdType.MESH
HIGH = lax.Precision.HIGHEST


def dot(a, b, over_a, over_b, precision=None):
    return lax.dot_general(
        a, b, (((over_a,), (over_b,)), ((), ())), precision=precision, preferred_element_type=F32
    )


def each_peer(count, me, body):
    for i in range(count - 1):
        offset = count // 2 + ((i + 1) // 2) * (1 - 2 * (i % 2))
        body(lax.rem(me + offset, count))


def near_places(steps):
    pairs = [(a, b) for a in range(X) for b in steps if (a, b) != (0, 0)]
    return sorted(pairs, key=lambda p: -(min(p[0], X - p[0]) + abs(p[1])))


def wait_for(ref, sem):
    pltpu.make_async_copy(ref, ref, sem).wait()


class Scan:
    def __init__(self, place, rate_ref, backward, refs):
        self.x, self.z, self.Z = place
        self.rate_ref = rate_ref
        self.backward = backward
        self.send, self.gather, self.inner, self.own, self.out, self.far, self.outer = refs[:7]
        self.back, self.result, self.sems = refs[7:]
        self.first = lax.rem(self.z + self.Z - 2, self.Z)
        self.shift = [(self.first + q) // self.Z for q in range(WINDOW)]
        self.ring = range(WINDOW, self.Z, WINDOW)

    def clear(self):
        zero = jnp.zeros((PIECE, HEAD), F32)
        for q in range(WINDOW):
            self.gather[q, 0] = zero.astype(BF16)
            self.gather[q, X + 1] = zero.astype(BF16)
        for j in range(len(self.ring)):
            for i in (0, 1, X + 1, X + 2):
                self.far[j, i] = zero.astype(BF16)
        self.own[0] = zero
        self.own[X + 2] = zero

    def piece(self, ref, x, z):
        start = (x * WINDOW + lax.rem(z, WINDOW)) * PIECE
        return ref.at[pl.ds(pl.multiple_of(start, PIECE), PIECE)]

    def decay(self, blocks):
        return jnp.exp(jnp.full((1, HEAD), -float(TOK * blocks) * self.rate_ref[self.x], F32))

    def copy(self, source, target, step, x, z):
        pltpu.make_async_remote_copy(
            src_ref=source,
            dst_ref=target,
            send_sem=self.sems.at[2 * step],
            recv_sem=self.sems.at[2 * step + 1],
            device_id={"ctx": x * self.Z + z},
            device_id_type=MESH,
        ).start()

    def at(self, a, b):
        return lax.rem(self.x + a, X), lax.rem(self.z + b + self.Z, self.Z)

    def wait_near(self, sem):
        wait_for(self.gather.at[pl.ds(0, 3), pl.ds(0, 5)], self.sems.at[sem])

    def wait_far(self, sem):
        wait_for(self.far.at[:, pl.ds(0, X)], self.sems.at[sem])

    def exchange(self):
        for a in (2, 1, 3, 0):
            self.exchange_with(a)
        self.keep()

    def exchange_with(self, a):
        for b in (2, 1, -1, 0):
            if (a, b) != (0, 0):
                x, z = self.at(a, b)
                self.copy(self.piece(self.send, x, z), self.gather.at[2 - b, self.x + 1], 0, x, z)

    def keep(self):
        self.gather[2, self.x + 1] = self.piece(self.send, self.x, self.z)[...]

    def total(self):
        decay, row_decay = self.decay(1), self.decay(self.Z)
        instances, slots = range(X + 1), range(WINDOW)
        if self.backward:
            instances, slots = instances[::-1], slots[::-1]
        self.wait_near(1)
        running = jnp.zeros((PIECE, HEAD), F32)
        for i in instances:
            state = jnp.zeros((PIECE, HEAD), F32)
            for q in slots:
                self.inner[i, q] = state
                state = decay * state + self.gather[q, i + self.shift[q]].astype(F32)
            running = row_decay * running + state
            self.own[i + 1] = running
            self.out[i] = running.astype(BF16)
        for j, distance in sorted(enumerate(self.ring), key=lambda p: -min(p[1], self.Z - p[1])):
            x, z = self.at(0, distance)
            start = 1 if self.backward else jnp.where(self.first + distance < self.Z, 1, 0)
            self.copy(self.out.at[pl.ds(start, X)], self.far.at[j, pl.ds(start + 1, X)], 1, x, z)

    def finish(self):
        gaps, offsets = [], []
        for distance in self.ring:
            if self.backward:
                gaps.append(self.decay(self.Z - distance - WINDOW))
                offsets.append(1 + jnp.where(self.first < distance, 0, 1))
            else:
                gaps.append(self.decay(distance - WINDOW))
                offsets.append(1 - jnp.where(self.first >= distance, 0, 1))
        own_gap = self.decay(self.Z - WINDOW)
        reach = [self.decay(WINDOW - 1 - q if self.backward else q) for q in range(WINDOW)]
        self.wait_far(3)
        for i in range(X + 1):
            total = own_gap * self.own[i + 2 if self.backward else i]
            for j, (gap, offset) in enumerate(zip(gaps, offsets)):
                total = total + gap * self.far[j, i + offset].astype(F32)
            self.outer[i] = total
        for x in range(X):
            for q in range(WINDOW):
                i = x + 1 - self.shift[q]
                self.back[x, q] = (reach[q] * self.outer[i] + self.inner[i, q]).astype(BF16)
        mine = self.piece(self.result, self.x, self.z)
        for a, b in near_places((-2, -1, 0, 1)):
            x, z = self.at(a, b)
            self.copy(self.back.at[x, b + 2], mine, 2, x, z)
        mine[...] = self.back[self.x, 2]

    def arrived(self):
        self.wait_near(5)

    def close(self):
        self.wait_near(0)
        self.wait_far(2)
        self.wait_near(4)


def kernel(
    Z,
    DP,
    rate_hbm,
    gain_hbm,
    q_hbm,
    k_hbm,
    v_hbm,
    cot_hbm,
    k,
    v,
    normed,
    gq,
    gk_part,
    gv_part,
    rest_weight,
    later_out,
    gg_ref,
    rate_ref,
    gain_ref,
    q,
    cot,
    grad,
    weighted,
    probs,
    dscore,
    mask,
    down_base,
    up_base,
    attn,
    cot_gain,
    norm_parts,
    gain_near,
    gain_far,
    gain_x,
    term,
    term_x,
    term_near,
    term_far,
    *rest,
):
    forward_refs, backward_refs = rest[0:10], rest[10:20]
    load_sems, small_sems, relay = rest[20:]
    ctx, d = lax.axis_index("ctx"), lax.axis_index("dp")
    x, z = ctx // Z, lax.rem(ctx, Z)
    channels = DP * WIDE
    share = WIDE // (X * Z)

    place = (x, z, Z)
    ahead = Scan(place, rate_ref, False, forward_refs)
    behind = Scan(place, rate_ref, True, backward_refs)
    incoming, later = ahead.result, behind.result
    ahead.clear()
    behind.clear()

    barrier = pltpu.get_barrier_semaphore()

    def ring(b):
        return lax.rem(z + b + Z, Z)

    far_steps = range(WINDOW, Z, WINDOW)
    near = near_places((2, 1, 0, -1, -2))
    for a, b in near:
        target = lax.rem(x + a, X) * Z + ring(b)
        pl.semaphore_signal(barrier, inc=1, device_id={"ctx": target}, device_id_type=MESH)

    def tell(n, steps):
        for b in (steps, -steps):
            pl.semaphore_signal(
                relay.at[n], inc=1, device_id={"ctx": x * Z + ring(b)}, device_id_type=MESH
            )

    def told(n):
        pl.semaphore_wait(relay.at[n], 2)

    def greet_dp(peer):
        pl.semaphore_signal(barrier, inc=1, device_id={"dp": peer}, device_id_type=MESH)

    each_peer(DP, d, greet_dp)

    sources = ((k_hbm, k), (v_hbm, v), (q_hbm, q), (cot_hbm, cot))
    small_loads = [
        pltpu.make_async_copy(rate_hbm, rate_ref, load_sems.at[4]),
        pltpu.make_async_copy(gain_hbm, gain_ref, load_sems.at[5]),
    ]
    for load in small_loads:
        load.start()
    for i, (source, target) in enumerate(sources):
        for b in range(BLOCKS):
            part = pl.ds(b * SUB, SUB)
            pltpu.make_async_copy(source.at[part], target.at[part], load_sems.at[i]).start()

    def loaded(i):
        wait_for(sources[i][1], load_sems.at[i])

    def lanes(h):
        return pl.ds(h * HEAD if isinstance(h, int) else pl.multiple_of(h * HEAD, HEAD), HEAD)

    def rows_of(b):
        return slice(b * SUB, (b + 1) * SUB)

    def scaled(h, count):
        return jnp.exp(jnp.full((1, HEAD), -float(count) * rate_ref[h], F32))

    row_index = lax.broadcasted_iota(jnp.int32, (SUB, HEAD), 0).astype(F32)

    def make_up(h):
        up_base[h] = jnp.exp(-rate_ref[h] * (SUB - 1.0 - row_index))

    def make_down(h):
        down_base[h] = jnp.exp(-rate_ref[h] * row_index)

    def up(h, b, extra=0):
        return up_base[h] * scaled(h, SUB * (BLOCKS - 1 - b) + extra)

    def down(h, b, extra=0):
        return down_base[h] * scaled(h, SUB * b + extra)

    def make_mask(h):
        t = lax.broadcasted_iota(jnp.int32, (HALF, HALF), 0)
        i = lax.broadcasted_iota(jnp.int32, (HALF, HALF), 1)
        offset = (t - i).astype(F32)
        near = jnp.exp(-rate_ref[h] * jnp.maximum(offset, 0.0))
        mask[h, 0] = jnp.where(t >= i, near, 0.0)
        mask[h, 1] = jnp.exp(-rate_ref[h] * (offset + float(HALF)))

    def block_state(h):
        weighted_k = jnp.concatenate(
            [
                (k[rows_of(b), lanes(h)].astype(F32) * up(h, b)).astype(BF16)
                for b in range(BLOCKS)
            ],
            axis=0,
        )
        state = dot(weighted_k, v[:, lanes(h)], 0, 0)
        ahead.send[pl.ds(h * HEAD, HEAD)] = state.astype(BF16)

    def masked(h, left, right, out):
        for tb in range(2):
            rows = slice(tb * HALF, (tb + 1) * HALF)
            for ib in range(tb + 1):
                cols = slice(ib * HALF, (ib + 1) * HALF)
                score = dot(left[rows, lanes(h)], right[cols, lanes(h)], 1, 1)
                out[h, rows, cols] = (score * mask[h, tb - ib]).astype(BF16)

    def below(table, h, right):
        return (
            dot(table[h, 0:HALF, 0:HALF], right[0:HALF, lanes(h)], 1, 0),
            dot(table[h, HALF:TOK, :], right[:, lanes(h)], 1, 0),
        )

    def above(table, h, right):
        return (
            dot(table[h, :, 0:HALF], right[:, lanes(h)], 0, 0),
            dot(table[h, HALF:TOK, HALF:TOK], right[HALF:TOK, lanes(h)], 0, 0),
        )

    def local_part(h):
        make_mask(h)
        masked(h, q, k, probs)
        first, second = below(probs, h, v)
        attn[0:HALF, lanes(h)] = first
        attn[HALF:TOK, lanes(h)] = second

    def weigh_queries(h):
        make_down(h)
        for b in range(BLOCKS):
            weighted_q = q[rows_of(b), lanes(h)].astype(F32) * down(h, b)
            weighted[h, :, rows_of(b)] = weighted_q.T.astype(BF16)
            rest_weight[h, rows_of(b)] = up(h, b, 1)

    def send_row(source, target, kind, peer_ctx):
        pltpu.make_async_remote_copy(
            src_ref=source,
            dst_ref=target,
            send_sem=small_sems.at[kind],
            recv_sem=small_sems.at[kind + 1],
            device_id={"ctx": peer_ctx},
            device_id_type=MESH,
        ).start()

    lane = lax.broadcasted_iota(jnp.int32, (1, HEAD), 1)

    def sum_of(ref):
        total = ref[0]
        for n in range(1, ref.shape[0]):
            total = total + ref[n]
        return total

    def sum_near(ref, kind):
        for n in range(1, WINDOW):
            send_row(ref.at[0], ref.at[n], kind, x * Z + ring(NEAR[n]))

    def sum_far(ref, kind):
        for n, b in enumerate(far_steps):
            send_row(ref.at[0], ref.at[n + 1], kind, x * Z + ring(b))

    def rows_arrived(ref, sem):
        wait_for(ref.at[pl.ds(0, ref.shape[0] - 1)], small_sems.at[sem])

    def gain_first():
        own = jnp.zeros((1, HEAD), F32)
        for n in range(share):
            own = jnp.where(lane == z * share + n, gain_ref[n], own)
        gain_near[0] = own
        sum_near(gain_near, 0)

    def gain_second():
        rows_arrived(gain_near, 1)
        gain_far[0] = sum_of(gain_near)
        sum_far(gain_far, 2)

    def gain_third():
        rows_arrived(gain_far, 3)
        gain_x[x] = sum_of(gain_far)
        each_peer(X, x, lambda peer: send_row(gain_x.at[x], gain_x.at[x], 4, peer * Z + z))

    small_loads[0].wait()
    for h in range(LOCAL):
        make_up(h)
    loaded(0)
    loaded(1)
    for h in range(LOCAL):
        block_state(h)
    small_loads[1].wait()
    pl.semaphore_wait(barrier, len(near) + DP - 1)
    tell(0, 2)
    ahead.exchange()
    gain_first()
    loaded(2)
    local_part(0)
    told(0)
    tell(1, 4)
    local_part(1)
    told(1)
    ahead.total()
    gain_second()
    local_part(2)
    local_part(3)
    for h in range(LOCAL):
        weigh_queries(h)
    loaded(3)
    ahead.finish()
    gain_third()
    rows_arrived(gain_x, 5)
    for h in range(LOCAL):
        for b in range(BLOCKS):
            at = (rows_of(b), lanes(h))
            cot_gain[at] = cot[at].astype(F32) * gain_x[h]
    factors = [[scaled(h, SUB * b + 1) for b in range(BLOCKS)] for h in range(LOCAL)]
    ahead.arrived()

    remote = [
        dot(q[:, lanes(h)], incoming[pl.ds(h * HEAD, HEAD)], 1, 0) for h in range(LOCAL)
    ]
    row8 = lax.broadcasted_iota(jnp.int32, (8, HEAD), 0)
    sums = jnp.zeros((8, HEAD), F32)
    for b in range(BLOCKS):
        square = jnp.zeros((SUB, HEAD), F32)
        cross = jnp.zeros((SUB, HEAD), F32)
        for h in range(LOCAL):
            at = (rows_of(b), lanes(h))
            a = attn[at] + down_base[h] * factors[h][b] * remote[h][rows_of(b)]
            attn[at] = a
            square = square + a * a
            cross = cross + cot_gain[at] * a
        sums = jnp.where(row8 == b, jnp.sum(square.T, axis=0, keepdims=True), sums)
        sums = jnp.where(row8 == b + BLOCKS, jnp.sum(cross.T, axis=0, keepdims=True), sums)
    norm_parts[d] = sums

    def send_norm(peer):
        pltpu.make_async_remote_copy(
            src_ref=norm_parts.at[d],
            dst_ref=norm_parts.at[d],
            send_sem=small_sems.at[12],
            recv_sem=small_sems.at[13],
            device_id={"dp": peer},
            device_id_type=MESH,
        ).start()

    each_peer(DP, d, send_norm)
    rows_arrived(norm_parts, 13)
    whole = norm_parts[0]
    for n in range(1, DP):
        whole = whole + norm_parts[n]
    inverse_rows = lax.rsqrt(whole[0:BLOCKS] / channels + eps_norm)
    cross_rows = inverse_rows * inverse_rows * inverse_rows * whole[BLOCKS : 2 * BLOCKS] / channels

    def column(rows, b):
        return jnp.broadcast_to(rows[b : b + 1], (SUB, HEAD)).T

    inverse = [column(inverse_rows, b) for b in range(BLOCKS)]
    cross_part = [column(cross_rows, b) for b in range(BLOCKS)]

    def back_state(h):
        for b in range(BLOCKS):
            at = (rows_of(b), lanes(h))
            grad[at] = (
                cot_gain[at] * inverse[b] - attn[at] * cross_part[b]
            ).astype(BF16)
        state = dot(weighted[h], grad[:, lanes(h)], 1, 0)
        behind.send[pl.ds(pl.multiple_of(h * HEAD, HEAD), HEAD)] = state.astype(BF16)

    def norm_out(h):
        total = jnp.zeros((1, HEAD), F32)
        for b in range(BLOCKS):
            at = (rows_of(b), lanes(h))
            scaled_attn = attn[at] * inverse[b]
            normed[at] = (scaled_attn * gain_x[h]).astype(BF16)
            total = total + jnp.sum(cot[at].astype(F32) * scaled_attn, axis=0, keepdims=True)
        term[h] = total

    def spread_term():
        each_peer(X, x, lambda peer: send_row(term.at[peer], term_x.at[x], 6, peer * Z + z))
        term_x[x] = term[x]

    def term_second():
        rows_arrived(term_x, 7)
        term_near[0] = sum_of(term_x)
        sum_near(term_near, 8)

    def term_third():
        rows_arrived(term_near, 9)
        term_far[0] = sum_of(term_near)
        sum_far(term_far, 10)

    def finish_term():
        rows_arrived(term_far, 11)
        whole = sum_of(term_far)
        source = lax.broadcasted_iota(jnp.int32, (HEAD, HEAD), 0)
        target = lax.broadcasted_iota(jnp.int32, (HEAD, HEAD), 1)
        pick = (source == target + z * share).astype(F32)
        mine = dot(jnp.broadcast_to(whole, (8, HEAD)), pick, 1, 0, HIGH)
        gg_ref[...] = mine[0:1, 0:share]

    def gradient_part(h):
        masked(h, grad, v, dscore)
        near = below(dscore, h, k)
        far = dot(grad[:, lanes(h)], incoming[pl.ds(h * HEAD, HEAD)], 1, 1)
        for b in range(BLOCKS):
            half, inner = divmod(b * SUB, HALF)
            gq[rows_of(b), lanes(h)] = (
                near[half][inner : inner + SUB] + down(h, b, 1) * far[rows_of(b)]
            ).astype(BF16)
        first, second = above(dscore, h, q)
        gk_part[0:HALF, lanes(h)] = first
        gk_part[HALF:TOK, lanes(h)] = second
        first, second = above(probs, h, grad)
        gv_part[0:HALF, lanes(h)] = first
        gv_part[HALF:TOK, lanes(h)] = second

    for a in (2, 1, 3, 0):
        h = lax.rem(x + a, LOCAL)
        back_state(h)
        behind.exchange_with(a)
    behind.keep()
    for h in range(LOCAL):
        norm_out(h)
    spread_term()
    gradient_part(0)
    gradient_part(1)
    behind.total()
    term_second()
    gradient_part(2)
    gradient_part(3)
    term_third()
    behind.finish()
    finish_term()
    behind.arrived()
    later_out[...] = later[...]

    ahead.close()
    behind.close()
    rows_arrived(gain_near, 0)
    rows_arrived(gain_far, 2)
    rows_arrived(gain_x, 4)
    rows_arrived(term_x, 6)
    rows_arrived(term_near, 8)
    rows_arrived(term_far, 10)
    rows_arrived(norm_parts, 12)


def writer(
    k,
    v,
    normed,
    gq,
    gk_part,
    gv_part,
    rest_weight,
    later,
    gain_sum,
    normed_hbm,
    gq_hbm,
    gk_hbm,
    gv_hbm,
    gg_hbm,
    gk,
    gv,
    sems,
):
    pltpu.make_async_copy(gain_sum, gg_hbm, sems.at[4]).start()

    def write(i, source, target, b):
        part = pl.ds(b * SUB, SUB)
        pltpu.make_async_copy(source.at[part], target.at[part], sems.at[i]).start()

    for b in range(BLOCKS):
        write(0, normed, normed_hbm, b)
        write(1, gq, gq_hbm, b)
    for b in range(BLOCKS):
        rows = slice(b * SUB, (b + 1) * SUB)
        for h in range(LOCAL):
            at = (rows, slice(h * HEAD, (h + 1) * HEAD))
            state = later[pl.ds(h * HEAD, HEAD)]
            weight = rest_weight[h, rows]
            gk[at] = (gk_part[at] + weight * dot(v[at], state, 1, 1)).astype(BF16)
            gv[at] = (gv_part[at] + weight * dot(k[at], state, 1, 0)).astype(BF16)
        write(2, gk, gk_hbm, b)
        write(3, gv, gv_hbm, b)
    for i, whole in enumerate((normed, gq, gk, gv, gain_sum)):
        wait_for(whole, sems.at[i])


def per_device(Z, DP, queries, keys, values, cotangent, log_decay, gain):
    owners = Z // WINDOW
    share = gain.shape[0]
    tokens = pltpu.VMEM((TOK, WIDE), BF16)
    square = pltpu.VMEM((LOCAL, TOK, TOK), BF16)
    scan = [
        pltpu.VMEM((WIDE, HEAD), BF16),
        pltpu.VMEM((WINDOW, X + 2, PIECE, HEAD), BF16),
        pltpu.VMEM((X + 1, WINDOW, PIECE, HEAD), F32),
        pltpu.VMEM((X + 3, PIECE, HEAD), F32),
        pltpu.VMEM((X + 1, PIECE, HEAD), BF16),
        pltpu.VMEM((owners - 1, X + 3, PIECE, HEAD), BF16),
        pltpu.VMEM((X + 1, PIECE, HEAD), F32),
        pltpu.VMEM((X, WINDOW, PIECE, HEAD), BF16),
        pltpu.VMEM((WIDE, HEAD), BF16),
        pltpu.SemaphoreType.DMA((6,)),
    ]
    half, full = jax.ShapeDtypeStruct((TOK, WIDE), BF16), jax.ShapeDtypeStruct((TOK, WIDE), F32)
    hbm = pl.BlockSpec(memory_space=pltpu.HBM)
    vmem = pl.BlockSpec(memory_space=pltpu.VMEM)
    inputs = [
        pltpu.with_memory_space_constraint(array, pltpu.HBM)
        for array in (log_decay, gain, queries, keys, values, cotangent)
    ]
    held = pl.pallas_call(
        functools.partial(kernel, Z, DP),
        out_shape=[
            half,
            half,
            half,
            half,
            full,
            full,
            jax.ShapeDtypeStruct((LOCAL, TOK, HEAD), F32),
            jax.ShapeDtypeStruct((WIDE, HEAD), BF16),
            jax.ShapeDtypeStruct((1, share), F32),
        ],
        in_specs=[hbm] * 6,
        out_specs=[vmem] * 9,
        scratch_shapes=[
            pltpu.SMEM((LOCAL,), F32),
            pltpu.SMEM((share,), F32),
            tokens,
            tokens,
            tokens,
            pltpu.VMEM((LOCAL, HEAD, TOK), BF16),
            square,
            square,
            pltpu.VMEM((LOCAL, 2, HALF, HALF), F32),
            pltpu.VMEM((LOCAL, SUB, HEAD), F32),
            pltpu.VMEM((LOCAL, SUB, HEAD), F32),
            pltpu.VMEM((TOK, WIDE), F32),
            pltpu.VMEM((TOK, WIDE), F32),
            pltpu.VMEM((DP, 8, HEAD), F32),
            pltpu.VMEM((WINDOW, 1, HEAD), F32),
            pltpu.VMEM((owners, 1, HEAD), F32),
            pltpu.VMEM((X, 1, HEAD), F32),
            pltpu.VMEM((LOCAL, 1, HEAD), F32),
            pltpu.VMEM((X, 1, HEAD), F32),
            pltpu.VMEM((WINDOW, 1, HEAD), F32),
            pltpu.VMEM((owners, 1, HEAD), F32),
        ]
        + scan
        + scan
        + [pltpu.SemaphoreType.DMA((6,)), pltpu.SemaphoreType.DMA((14,)), pltpu.SemaphoreType.REGULAR((2,))],
        compiler_params=pltpu.CompilerParams(
            collective_id=0, has_side_effects=True, vmem_limit_bytes=40 * 1024 * 1024
        ),
        cost_estimate=pl.CostEstimate(
            flops=2_000_000_000, bytes_accessed=4_200_000, transcendentals=700_000
        ),
    )(*inputs)
    normed, gq, gk, gv, gg = pl.pallas_call(
        writer,
        out_shape=[half, half, half, half, jax.ShapeDtypeStruct((1, share), F32)],
        in_specs=[vmem] * 9,
        out_specs=[hbm] * 5,
        scratch_shapes=[tokens, tokens, pltpu.SemaphoreType.DMA((5,))],
        compiler_params=pltpu.CompilerParams(vmem_limit_bytes=24 * 1024 * 1024),
        cost_estimate=pl.CostEstimate(
            flops=300_000_000, bytes_accessed=2_200_000, transcendentals=0
        ),
    )(*held)
    return normed, gq, gk, gv, gg.reshape(share)


def solution(mesh):
    both = P("ctx", "dp")
    return jax.shard_map(
        functools.partial(per_device, mesh.shape["ctx"] // X, mesh.shape["dp"]),
        mesh=mesh,
        in_specs=(both, both, both, both, P("dp"), P(("dp", "ctx"))),
        out_specs=(both, both, both, both, P(("dp", "ctx"))),
        check_vma=False,
    )
```
